256 devices in a mesh: dp: 32 (over z, x), vocab: 8 (over y, core).
Axes of the slice: x: 4, y: 4, z: 8, core: 2. Of those that a mesh axis runs over, the one named last changes fastest.
Arguments:
- hidden: bfloat16 [24576, 4096], P('dp'), may hold values from -8 to 8
- out_embed: bfloat16 [4096, 16384], P('dp', 'vocab'), may hold values from -1 to 1
- key_proj: bfloat16 [4096, 128], replicated, may hold values from -0.09375 to 0.09375
- targets: int32 [24576], P('dp'), may hold values from 0 to 16383
- doc_ids: int32 [24576], P('dp'), may hold values from 0 to 1
- list_owner: int32 [32, 64], P('dp'), may hold values from 0 to 31, as said below
- list_block: int32 [32, 64], P('dp'), may hold values from 0 to 5, as said below
- list_count: int32 [32], P('dp'), may hold values from 8 to 64, as said below
Outputs:
- row_loss: float32 [24576], P('dp')
The draws below stay inside these ranges and needn't reach their ends.
Inputs may be any that keep to these rules, and one draw needn't show every extreme that they name: `list_owner`: among the first list_count[d] slots of row d at most 2 name the same owner; a row whose count is 64 names every owner exactly 2 times. Slots from list_count[d] on are ignored. `list_block`: live slots of one row that name the same owner name different blocks. `list_count`: some device's count is 64 in every draw.
All inputs are finite; a program needn't handle non-finite values.
Results may differ from the reference program's by a relative error of at most 0.0015.
Values may be sent and summed in bfloat16 or wider, within the bound.
A program may use at most 128 MiB of HBM per device.

```python
import math
import jax
import jax.numpy as jnp
import numpy as np
from jax import lax

D = 4096
VOCAB = 16384
KD = 128
KB = 128
TOK_DEV = 768
NB = 6
SLOTS = 64
TOKENS = 24576
N_DP = 32


def embed_table(key):
    table = jax.random.normal(jax.random.fold_in(key, 31), (D, VOCAB), jnp.float32)
    return jnp.clip(table * (2.0 / math.sqrt(D)), -1.0, 1.0)


def draw_out_embed(key, part):
    table = embed_table(key)
    return table.astype(jnp.bfloat16)


def draw_hidden(key, part):
    key = jax.random.fold_in(key, 3)
    subkeys = jax.random.split(key, 2)
    values = jax.random.normal(subkeys[1], (TOKENS, D), jnp.float32)
    return jnp.clip(values, -8.0, 8.0).astype(jnp.bfloat16)


def draw_doc_ids(key, part):
    key = jax.random.fold_in(key, 13)
    return jax.random.randint(key, (TOKENS,), 0, 2).astype(jnp.int32)


def list_layout(key):
    owner_key, block_key = jax.random.split(jax.random.fold_in(key, 71))
    owner_score = jax.random.randint(owner_key, (N_DP, SLOTS), 0, 1 << 20) * SLOTS + jnp.arange(SLOTS, dtype=jnp.int32)[None, :]
    copies = jnp.argsort(owner_score, axis=1).astype(jnp.int32)
    owners = copies % N_DP
    copy_rank = copies // N_DP
    block_score = jax.random.randint(block_key, (N_DP, N_DP, NB), 0, 1 << 20) * NB + jnp.arange(NB, dtype=jnp.int32)
    block_order = jnp.argsort(block_score, axis=2).astype(jnp.int32)
    device_ids = jnp.arange(N_DP, dtype=jnp.int32)[:, None]
    blocks = block_order[device_ids, owners, copy_rank]
    return (owners.astype(jnp.int32), blocks.astype(jnp.int32))


def draw_list_owner(key, part):
    owners, blocks = list_layout(key)
    return owners


def draw_list_block(key, part):
    owners, blocks = list_layout(key)
    return blocks


def draw_list_count(key, part):
    key = jax.random.fold_in(key, 9)
    power_key, full_key = jax.random.split(key)
    powers = jax.random.randint(power_key, (N_DP,), 0, 4)
    counts = jnp.right_shift(jnp.full((N_DP,), SLOTS, jnp.int32), powers)
    fullest = jax.random.randint(full_key, (), 0, N_DP)
    return jnp.where(jnp.arange(N_DP) == fullest, SLOTS, counts).astype(jnp.int32)


def with_ends(values, stream_key, least, top_value):
    extent = values.shape
    index_at = [jax.random.randint(jax.random.fold_in(stream_key, axis), (), 0, extent[axis]) for axis in range(len(extent))]
    values = values.at[tuple(index_at)].set(least)
    longest = extent.index(max(extent))
    index_at[longest] = (index_at[longest] + 1) % extent[longest]
    return values.at[tuple(index_at)].set(top_value)


def rank_bounds(count, skew):
    portions = [(1 << 20) // math.isqrt(rank ** skew) + 1 for rank in range(1, count + 1)]
    deviation = 1 + sum(portions) // (1 << 30)
    return np.cumsum(np.array([max(1, weight // deviation) for weight in portions]))


def skewed_ids(key, extent, count, lean):
    listing = rank_bounds(count, lean)
    pick = jax.random.randint(jax.random.fold_in(key, 1), extent, 0, int(listing[count - 1]))
    standing = jnp.searchsorted(jnp.asarray(listing, jnp.int32), pick, side="right")
    return jax.random.permutation(jax.random.fold_in(key, 2), count)[standing].astype(jnp.int32)


def normal_values(own_key, dims, deviation, bound, kind=jnp.bfloat16):
    return jnp.clip(deviation * jax.random.normal(own_key, dims, jnp.float32), -bound, bound).astype(kind)


def setup_inputs(seed: int = 0) -> dict:
    seeds = jax.random.split(jax.random.key(seed), 9)
    return {
        "hidden": draw_hidden(jax.random.fold_in(seeds[8], 71), 0),
        "out_embed": draw_out_embed(jax.random.fold_in(seeds[8], 71), 0),
        "key_proj": normal_values(seeds[2], (D, KD), D ** -0.5, 0.09375),
        "targets": with_ends(skewed_ids(seeds[3], (TOKENS,), VOCAB, 2), jax.random.fold_in(seeds[3], 3), 0, VOCAB - 1).astype(jnp.int32),
        "doc_ids": draw_doc_ids(jax.random.fold_in(seeds[8], 71), 0),
        "list_owner": draw_list_owner(jax.random.fold_in(seeds[8], 71), 0),
        "list_block": draw_list_block(jax.random.fold_in(seeds[8], 71), 0),
        "list_count": draw_list_count(jax.random.fold_in(seeds[8], 71), 0),
    }


negative_fill = -1.0e30
score_base = 3.0


def reference(hidden, out_embed, key_proj, targets, doc_ids, list_owner, list_block, list_count):
    sim_scale = score_base / (KD ** 0.5)
    key_rows = jnp.dot(hidden, key_proj, preferred_element_type=jnp.float32).astype(jnp.bfloat16)
    block_rows = key_rows.reshape(N_DP * NB, KB, KD)
    block_tgt = targets.reshape(N_DP * NB, KB)
    block_doc = doc_ids.reshape(N_DP * NB, KB)
    offsets = jnp.arange(KB, dtype=jnp.int32)

    def one_device(inputs):
        device, row_data, row_keys, row_tgt, row_doc, owners, blocks, live_count = inputs
        logits = jnp.dot(row_data, out_embed, preferred_element_type=jnp.float32)
        slot_ids = owners * NB + blocks
        mem_rows = block_rows[slot_ids].reshape(SLOTS * KB, KD)
        mem_tgt = block_tgt[slot_ids].reshape(SLOTS * KB)
        mem_doc = block_doc[slot_ids].reshape(SLOTS * KB)
        mem_pos = (slot_ids[:, None] * KB + offsets[None, :]).reshape(SLOTS * KB)
        mem_live = jnp.repeat(jnp.arange(SLOTS, dtype=jnp.int32) < live_count, KB)
        row_pos = device * TOK_DEV + jnp.arange(TOK_DEV, dtype=jnp.int32)
        scores = sim_scale * jnp.dot(row_keys, mem_rows.T, preferred_element_type=jnp.float32)
        keep_mask = mem_live[None, :] & (mem_doc[None, :] == row_doc[:, None]) & (mem_pos[None, :] != row_pos[:, None])
        peak_value = jnp.maximum(jnp.max(logits, axis=1), jnp.max(jnp.where(keep_mask, scores, negative_fill), axis=1))
        mass_value = jnp.sum(jnp.exp(logits - peak_value[:, None]), axis=1)
        mass_value = mass_value + jnp.sum(jnp.exp(jnp.where(keep_mask, scores - peak_value[:, None], negative_fill)), axis=1)
        picked = jnp.take_along_axis(logits, row_tgt[:, None], axis=1)[:, 0]
        hit_mask = keep_mask & (mem_tgt[None, :] == row_tgt[:, None])
        hit_peak = jnp.maximum(picked, jnp.max(jnp.where(hit_mask, scores, negative_fill), axis=1))
        hit_mass = jnp.exp(picked - hit_peak)
        hit_mass = hit_mass + jnp.sum(jnp.exp(jnp.where(hit_mask, scores - hit_peak[:, None], negative_fill)), axis=1)
        return peak_value + jnp.log(mass_value) - hit_peak - jnp.log(hit_mass)

    devices = jnp.arange(N_DP, dtype=jnp.int32)
    losses = lax.map(one_device, (devices, hidden.reshape(N_DP, TOK_DEV, D), key_rows.reshape(N_DP, TOK_DEV, KD),
                                  targets.reshape(N_DP, TOK_DEV), doc_ids.reshape(N_DP, TOK_DEV),
                                  list_owner, list_block, list_count))
    return losses.reshape(TOKENS)
```

```python
import jax
import jax.numpy as jnp
from jax import lax
from jax.experimental import pallas as pl
from jax.experimental.pallas import tpu as pltpu
from jax.sharding import PartitionSpec as P

MESH = pl.DeviceIdType.MESH
NEG = -1e30
SCALE = 3.0 / 128**0.5
NX, NY, NZ = 4, 4, 8
CHUNK = 32
F32 = jnp.float32
BF16 = jnp.bfloat16


def kernel(
    hid, emb, kproj, tgt, doc, lown, lblk, lcnt, out,
    hb, eb, kp, lg, kv, mt, om, kg, kt, kd, ko, ms, st, r1, st2, r2,
    loc_sem, xe_s, xe_r, zp_s, zp_r, zm_s, zm_r, dc_s, dc_r,
    hx_s, hf_s, hx_r, yp_s, ym_s, yp_r, ym_r, yf_s, yf_r,
    kv_s, kv_r, om_s, om_r, kc_s, kc_r, mt_s, mt_r, r1_s, r1_r, r2_s, r2_r,
):
    d = lax.axis_index("dp")
    v = lax.axis_index("vocab")
    z, x = d // NX, d % NX
    y, c = v // 2, v % 2
    owner_here = z % NY == y
    first, second = c == 0, c == 1

    def tok_x(s):
        return (x + 3 * c + 2 * s) % NX

    def dev(dz, dx, dy, dc):
        return (((z + dz) % NZ) * NX + (x + dx) % NX, ((y + dy) % NY) * 2 + (c + dc) % 2)

    def rcopy(src, dst, ssem, rsem, to):
        return pltpu.make_async_remote_copy(
            src_ref=src, dst_ref=dst, send_sem=ssem, recv_sem=rsem, device_id=to, device_id_type=MESH
        )

    bar = pltpu.get_barrier_semaphore()
    for to in [dev(1, 0, 0, 0), dev(NZ - 1, 0, 0, 0)] + [
        dev(0, 1, 0, 0), dev(0, 2, 0, 0), dev(0, 3, 0, 0), dev(0, 1, 0, 1), dev(0, 3, 0, 1)
    ]:
        pl.semaphore_signal(bar, inc=1, device_id=to, device_id_type=MESH)
    for n in range(1, 8):
        pl.semaphore_signal(bar, inc=1, device_id=(d, (v + n) % 8), device_id_type=MESH)

    om_loads = []
    for n in range(6):
        om_loads.append(pltpu.make_async_copy(tgt.at[pl.ds(n * 128, 128)], om.at[2, n], loc_sem.at[4]))
        om_loads.append(pltpu.make_async_copy(doc.at[pl.ds(n * 128, 128)], om.at[2, 6 + n], loc_sem.at[4]))
    for cp in om_loads:
        cp.start()
    emb_loads = []
    for ph in range(2):
        col = pl.multiple_of(x * 512 + ph * 256, 256)
        cp = pltpu.make_async_copy(
            emb.at[:, pl.ds(col, 256)], eb.at[ph, c, pl.ds(pl.multiple_of(d * 128, 128), 128)], loc_sem.at[2 + ph]
        )
        cp.start()
        emb_loads.append(cp)
    own_slot = 2 * c
    kp_load = pltpu.make_async_copy(kproj, kp, loc_sem.at[1])
    kp_load.start()
    hid_load = pltpu.make_async_copy(hid, hb.at[own_slot], loc_sem.at[0])
    hid_load.start()
    om[2, 12:16] = jnp.zeros((4, 128), jnp.int32)
    om[2, 12:13, 0:64] = lown[...]
    om[2, 13:14, 0:64] = lblk[...]
    om[2, 14:15] = jnp.full((1, 128), lcnt[0], jnp.int32)
    pl.semaphore_wait(bar, 14)

    def eslot(ph, zz, i):
        row = ((zz % NZ) * NX + (x + i) % NX) * 128
        return eb.at[ph, c, pl.ds(pl.multiple_of(row, 128), 128)]

    def xe(ph, e):
        col = pl.multiple_of(((x + e) % NX) * 512 + ph * 256, 256)
        return rcopy(
            emb.at[:, pl.ds(col, 256)],
            eb.at[ph, c, pl.ds(pl.multiple_of(d * 128, 128), 128)],
            xe_s.at[ph, e], xe_r.at[ph, 4 - e], dev(0, e, 0, 0),
        )

    def xe_in(ph, i):
        return rcopy(
            emb.at[:, pl.ds(0, 256)], eslot(ph, z, i), xe_s.at[ph, i], xe_r.at[ph, i], dev(0, i, 0, 0)
        )

    def zplus(ph, s, i):
        ref = eslot(ph, z - (s - 1) + NZ, i)
        return rcopy(ref, ref, zp_s.at[ph, s - 1, i], zp_r.at[ph, s - 1, i], dev(1, 0, 0, 0))

    def zminus(ph, s, i):
        ref = eslot(ph, z + (s - 1), i)
        return rcopy(ref, ref, zm_s.at[ph, s - 1, i], zm_r.at[ph, s - 1, i], dev(NZ - 1, 0, 0, 0))

    def zplus_in(ph, s, i):
        ref = eslot(ph, z - s + NZ, i)
        return rcopy(ref, ref, zp_s.at[ph, s - 1, i], zp_r.at[ph, s - 1, i], dev(1, 0, 0, 0))

    def zminus_in(ph, s, i):
        ref = eslot(ph, z + s, i)
        return rcopy(ref, ref, zm_s.at[ph, s - 1, i], zm_r.at[ph, s - 1, i], dev(NZ - 1, 0, 0, 0))

    def d2d(ph, zz, n, shard):
        ref = eb.at[ph, shard, pl.ds(pl.multiple_of((zz % NZ) * 512, 512), 512)]
        return rcopy(ref, ref, dc_s.at[ph, n], dc_r.at[ph, n], dev(0, 0, 0, 1))

    d2d_z = [0, 7, 6, 5, 1, 2, 3, 4]

    def z_first(ph, pair):
        for i in ((0,), (1,), (2, 3))[pair]:
            if i == 0:
                emb_loads[ph].wait()
            else:
                xe_in(ph, i).wait_recv()
            zplus(ph, 1, i).start()
            zminus(ph, 1, i).start()
        if pair == 2:
            d2d(ph, z, 0, c).start()

    def z_event(ph, s, pair):
        if s < 4:
            for i in (0, 1) if pair == 0 else (2, 3):
                zplus_in(ph, s, i).wait_recv()
                if s < 3 or i < 2:
                    zplus(ph, s + 1, i).start()
                zminus_in(ph, s, i).wait_recv()
                if s < 3 or i >= 2:
                    zminus(ph, s + 1, i).start()
            if pair == 1:
                d2d(ph, z + NZ - s, s, c).start()
                d2d(ph, z + s, 3 + s, c).start()
        else:
            for i in (0, 1):
                zplus_in(ph, 4, i).wait_recv()
                zminus_in(ph, 4, i + 2).wait_recv()
            d2d(ph, z + 4, 7, c).start()

    def embed_ready(ph):
        for n in range(8):
            d2d(ph, z + d2d_z[n], n, 1 - c).wait_recv()

    def rows_of(j, yy):
        b, k = j // 4, j % 4
        if b == 0:
            return pl.ds(pl.multiple_of(256 + (yy % NY) * 128 + k * CHUNK, CHUNK), CHUNK)
        return pl.ds((b - 1) * 128 + k * CHUNK, CHUNK)

    right, left = dev(0, 1, 0, 1), dev(0, 3, 0, 1)

    def hx_own(j, s):
        r = rows_of(j, y)
        return rcopy(hid.at[r], hb.at[s, r], hx_s.at[s, j], hx_r.at[s, j], (right, left)[s])

    def hx_fwd(j):
        r = rows_of(j, y)
        s = 0 if j % 4 < 2 else 1
        return rcopy(hb.at[s, r], hb.at[1, r], hf_s.at[j], hx_r.at[1, j], (right, left)[s])

    def hx_in(j, s):
        r = rows_of(j, y)
        return rcopy(hb.at[s, r], hb.at[s, r], hf_s.at[j], hx_r.at[s, j], right)

    def yown(s, k, up):
        r = rows_of(k, y)
        if up:
            return rcopy(hb.at[s, r], hb.at[s, r], yp_s.at[s, k], yp_r.at[s, k], dev(0, 0, 1, 0))
        return rcopy(hb.at[s, r], hb.at[s, r], ym_s.at[s, k], ym_r.at[s, k], dev(0, 0, 3, 0))

    def yin(s, k, up):
        if up:
            r = rows_of(k, y + 3)
            return rcopy(hb.at[s, r], hb.at[s, r], yp_s.at[s, k], yp_r.at[s, k], dev(0, 0, 1, 0))
        r = rows_of(k, y + 1)
        return rcopy(hb.at[s, r], hb.at[s, r], ym_s.at[s, k], ym_r.at[s, k], dev(0, 0, 3, 0))

    def yfwd(s, k):
        if k < 2:
            r = rows_of(k, y + 3)
            return rcopy(hb.at[s, r], hb.at[s, r], yf_s.at[s, k], yf_r.at[s, k], dev(0, 0, 1, 0))
        r = rows_of(k, y + 1)
        return rcopy(hb.at[s, r], hb.at[s, r], yf_s.at[s, k], yf_r.at[s, k], dev(0, 0, 3, 0))

    def yfwd_in(s, k):
        r = rows_of(k, y + 2)
        return rcopy(hb.at[s, r], hb.at[s, r], yf_s.at[s, k], yf_r.at[s, k], dev(0, 0, 1, 0))

    def x_send(j):
        @pl.when(first)
        def _():
            hx_own(j, 0).start()
            hx_own(j, 1).start()

    def x_near(j):
        @pl.when(second)
        def _():
            for s in range(2):
                hx_in(j, s).wait_recv()
            if j < 4:
                hx_fwd(j).start()
                for s in range(2):
                    yown(s, j, True).start()
                    yown(s, j, False).start()

    def x_forward(*js):
        @pl.when(second)
        def _():
            for j in js:
                hx_fwd(j).start()

    def x_far(*js):
        @pl.when(first)
        def _():
            for j in js:
                hx_in(j, 1).wait_recv()
                if j < 4:
                    yown(1, j, True).start()
                    yown(1, j, False).start()

    def y_recv_of(s, k):
        yin(s, k, True).wait_recv()
        if k < 2:
            yfwd(s, k).start()
        yin(s, k, False).wait_recv()
        if k >= 2:
            yfwd(s, k).start()

    def y_near(k):
        @pl.when(second)
        def _():
            y_recv_of(1, k)
            y_recv_of(0, k)

    def y_far(k):
        @pl.when(first)
        def _():
            y_recv_of(1, k)

    def y_last(k):
        yfwd_in(1, k).wait_recv()

        @pl.when(second)
        def _():
            yfwd_in(0, k).wait_recv()

    my_owner = z // NY
    half = pl.ds(pl.multiple_of(c * 384, 384), 384)
    up, down = dev(1, 0, 0, 0), dev(NZ - 1, 0, 0, 0)

    def key_copy(o, n, to):
        return rcopy(kv.at[o, half], kv.at[o, half], kv_s.at[o, n], kv_r.at[o], to)

    def int_copy(o, n, to):
        return rcopy(om.at[o], om.at[o], om_s.at[o, n], om_r.at[o], to)

    def key_cross(o):
        return rcopy(kv.at[o, half], kv.at[o, half], kc_s.at[o], kc_r.at[o], dev(0, 0, 0, 1))

    def key_cross_in(o):
        ref = kv.at[o, pl.ds(pl.multiple_of(384 - c * 384, 384), 384)]
        return rcopy(ref, ref, kc_s.at[o], kc_r.at[o], dev(0, 0, 0, 1))

    def mt_send(n):
        to, s = ((dev(0, 2, 0, 0), 1), (right, 0), (left, 1))[n]
        return rcopy(om.at[2], mt.at[s], mt_s.at[n], mt_r.at[s], to)

    def small_sends():
        for cp in om_loads:
            cp.wait()

        @pl.when(first)
        def _():
            for n in range(3):
                mt_send(n).start()
            mt[0] = om[2]

    def key_sends():
        hid_load.wait()
        kp_load.wait()

        @pl.when(owner_here)
        def _():
            kv[my_owner, half, :] = jnp.dot(
                hb[own_slot, half, :], kp[...], preferred_element_type=F32
            ).astype(BF16)
            om[my_owner] = om[2]
            key_cross(my_owner).start()
            for n, to in enumerate((up, down)):
                key_copy(my_owner, n, to).start()
                int_copy(my_owner, n, to).start()

    def hops(o):
        return (z - y - NY * o + 2 * NZ) % NZ

    def key_relay(hop):
        for o in range(2):
            key_relay_of(o, hop)

    def key_relay_of(o, hop):
        @pl.when((hops(o) == hop) | ((hops(o) == NZ - hop) & (hop < 4)))
        def _():
            key_copy(o, 0, up).wait_recv()
            int_copy(o, 0, up).wait_recv()
            key_cross(o).start()

        if hop < 4:
            @pl.when(hops(o) == hop)
            def _():
                key_copy(o, 0, up).start()
                int_copy(o, 0, up).start()

        if hop < 3:
            @pl.when(hops(o) == NZ - hop)
            def _():
                key_copy(o, 1, down).start()
                int_copy(o, 1, down).start()

    def keys_sent(o):
        @pl.when(hops(o) < 4)
        def _():
            key_copy(o, 0, up).wait_send()
            int_copy(o, 0, up).wait_send()

        @pl.when((hops(o) > 5) | (hops(o) == 0))
        def _():
            key_copy(o, 1, down).wait_send()
            int_copy(o, 1, down).wait_send()

        key_cross(o).wait_send()

    def memory_ready():
        for o in range(2):
            key_cross_in(o).wait_recv()

        rcopy(om.at[2], mt.at[1], mt_s.at[0], mt_r.at[1], right).wait_recv()

        @pl.when(second)
        def _():
            rcopy(om.at[2], mt.at[0], mt_s.at[0], mt_r.at[0], right).wait_recv()

        lane = lax.broadcasted_iota(jnp.int32, (1, 128), 1)
        for s in range(2):
            live = lane < mt[s, 14:15, :]
            for o in range(2):
                owner_id = (y + NY * o) * NX + x
                named = live & (mt[s, 12:13, :] == owner_id)
                blocks = mt[s, 13:14, :].astype(F32)
                most = jnp.max(jnp.where(named, blocks, -1.0), axis=1, keepdims=True)
                least = jnp.min(jnp.where(named, blocks, 99.0), axis=1, keepdims=True)
                least = jnp.where(least == most, 99.0, least)
                mine = jnp.where(owner_id == z * NX + tok_x(s), 1.0, 0.0)
                for k, at_block in enumerate((most, least)):
                    n = 2 * o + k
                    keys = jnp.zeros((128, 128), F32)
                    tgts, docs = jnp.zeros((1, 128), F32), jnp.full((1, 128), -1.0, F32)
                    for b in range(6):
                        w = jnp.where(at_block == float(b), 1.0, 0.0)
                        keys = keys + w * kv[o, b * 128 : b * 128 + 128, :].astype(F32)
                        tgts = tgts + w * om[o, b : b + 1, :].astype(F32)
                        docs = docs + w * (om[o, 6 + b : 7 + b, :].astype(F32) + 1.0)
                    kg[s, n * 128 : n * 128 + 128, :] = keys.astype(BF16)
                    kt[s, n : n + 1, :] = tgts
                    kd[s, n : n + 1, :] = docs
                    ko[s, n : n + 1, :] = jnp.broadcast_to(mine * (at_block + 1.0) - 1.0, (1, 128))

    def column(s, row):
        return jnp.broadcast_to(mt[s, pl.ds(row, 1), :].astype(F32), (128, 128)).T

    def rows_at(blk):
        return pl.ds(pl.multiple_of(blk * 128, 128), 128)

    def two_blocks(sa, ba, sb, bb):
        return jnp.concatenate([hb[sa, rows_at(ba), :], hb[sb, rows_at(bb), :]], axis=0)

    def scores(sa, ba, sb, bb):
        qs = jnp.dot(two_blocks(sa, ba, sb, bb), kp[...], preferred_element_type=F32).astype(BF16)
        scores_of(sa, ba, rows_at(ba), qs[:128])
        scores_of(sb, bb, rows_at(bb), qs[128:])

    def scores_of(s, blk, r, q):
        tcol = column(s, blk)
        dcol = column(s, 6 + blk)
        i0 = lax.broadcasted_iota(jnp.int32, (128, 128), 0)
        i1 = lax.broadcasted_iota(jnp.int32, (128, 128), 1)
        eye = i0 == i1
        sc = SCALE * lax.dot_general(q, kg[s], (((1,), (1,)), ((), ())), preferred_element_type=F32)
        kept, hits = [], []
        for n in range(4):
            mine = jnp.where(ko[s, n : n + 1, :] == blk.astype(F32), 2.0, 0.0)
            keep = kd[s, n : n + 1, :] == dcol + jnp.where(eye, mine, 0.0)
            sk = jnp.where(keep, sc[:, n * 128 : n * 128 + 128], NEG)
            kept.append(sk)
            hits.append(jnp.where(kt[s, n : n + 1, :] == tcol, sk, NEG))

        def stats(tiles):
            top = tiles[0]
            for t in tiles[1:]:
                top = jnp.maximum(top, t)
            top = jnp.max(top, axis=1, keepdims=True)
            total = jnp.exp(tiles[0] - top)
            for t in tiles[1:]:
                total = total + jnp.exp(t - top)
            return top, jnp.sum(total, axis=1, keepdims=True)

        mp, mm = stats(kept)
        hp, hm = stats(hits)
        ms[s, r, :] = jnp.where(i1 == 4, mp, jnp.where(i1 == 5, mm, jnp.where(i1 == 6, hp, hm)))

    def logits(sa, ba, sb, bb, ph):
        a = two_blocks(sa, ba, sb, bb)
        for cs in range(2):
            res = jnp.dot(a, eb[ph, cs], preferred_element_type=F32)
            cols = slice(ph * 512 + cs * 256, ph * 512 + cs * 256 + 256)
            lg[sa, rows_at(ba), cols] = res[:128]
            lg[sb, rows_at(bb), cols] = res[128:]

    def finish(s, blk):
        r = pl.ds(pl.multiple_of(blk * 128, 128), 128)
        tcol = column(s, blk)
        i1 = lax.broadcasted_iota(jnp.int32, (128, 128), 1)
        lane = lax.broadcasted_iota(jnp.int32, (1, 128), 1)
        tiles = [lg[s, r, n * 128 : n * 128 + 128] for n in range(8)]
        top = tiles[0]
        for t in tiles[1:]:
            top = jnp.maximum(top, t)
        top = jnp.max(top, axis=1, keepdims=True)
        total, pick = None, None
        for n in range(8):
            ph, cs, half = n // 4, (n // 2) % 2, n % 2
            base = (2 * y + cs) * 2048 + x * 512 + ph * 256 + half * 128
            e = jnp.exp(tiles[n] - top)
            total = e if total is None else total + e
            h = jnp.where((lane + base).astype(F32) == tcol, tiles[n], NEG)
            pick = h if pick is None else jnp.maximum(pick, h)
        total = jnp.sum(total, axis=1, keepdims=True)
        pick = jnp.max(pick, axis=1, keepdims=True)
        tile = jnp.where(i1 == 0, top, jnp.where(i1 == 1, total, jnp.where(i1 == 2, pick, ms[s, r, :])))
        t = tile.T
        lp, lm, lh = t[0:1], t[1:2], t[2:3]
        mp, mm, hp, hm = t[4:5], t[5:6], t[6:7], t[7:8]
        peak = jnp.maximum(lp, mp)
        hit = jnp.maximum(lh, hp)
        st[s, 0, pl.ds(blk, 1), :] = peak
        st[s, 1, pl.ds(blk, 1), :] = lm * jnp.exp(lp - peak) + mm * jnp.exp(mp - peak)
        st[s, 2, pl.ds(blk, 1), :] = hit
        st[s, 3, pl.ds(blk, 1), :] = jnp.exp(lh - hit) + hm * jnp.exp(hp - hit)

    def finish2(sa, ba, sb, bb):
        finish(sa, ba)
        finish(sb, bb)

    for e in range(1, 4):
        xe(0, e).start()
    z_first(0, 0)
    z_first(1, 0)
    x_send(0)
    x_send(1)
    for e in range(1, 4):
        xe(1, e).start()
    small_sends()
    for j in range(2, 12):
        x_send(j)
    key_sends()
    z_first(0, 1)
    z_first(0, 2)

    z_events = [(ph, s, q) for ph in range(2) for s in range(1, 5) for q in range(2 if s < 4 else 1)]
    qy, qd, qu, qo = 2 + y, 2 + (y + 3) % 4, 2 + (y + 1) % 4, 2 + (y + 2) % 4
    plan = {}

    def at(u, fn, *args):
        plan.setdefault(u, []).append((fn, args))

    for n, ev in enumerate(z_events):
        at(n, z_event, *ev)
    at(4, z_first, 1, 1)
    at(5, z_first, 1, 2)
    for j, u in enumerate((0, 1, 3, 4, 6, 7, 8, 9, 10, 11, 12, 13)):
        at(u, x_near, j)
    for u, js in ((11, (4, 6)), (12, (5, 7)), (13, (8, 10)), (14, (9, 11))):
        at(u, x_forward, *js)
    for u, js in ((4, (0,)), (5, (1,)), (7, (2,)), (8, (3,)), (15, (4, 6)), (16, (5, 7)), (17, (8, 10)), (18, (9, 11))):
        at(u, x_far, *js)
    for k in range(4):
        at((6, 8, 10, 12)[k], y_near, k)
        at((9, 10, 11, 12)[k], y_far, k)
        at((15, 17, 16, 18)[k], y_last, k)
    for hop, u in ((1, 1), (2, 3), (3, 5), (4, 7)):
        at(u, key_relay, hop)
    groups = [
        [jnp.where(first, a, b) for a, b in zip(on_first, on_second)]
        for on_first, on_second in (
            ((0, 0, 0, 1), (0, qy, 1, qy)),
            ((0, qy, 0, qd), (0, 0, 1, 0)),
            ((0, qu, 0, qo), (0, qd, 1, qd)),
            ((1, qd, 1, qu), (0, qu, 1, qu)),
            ((1, qy, 1, 0), (0, 1, 1, 1)),
            ((1, 1, 1, qo), (0, qo, 1, qo)),
        )
    ]
    at(8, embed_ready, 0)
    at(9, memory_ready)
    for n, u in enumerate((8, 10, 12, 13)):
        at(u, logits, *groups[n], 0)
        at(max(u, 9), scores, *groups[n])
    at(14, embed_ready, 1)
    for n, u in enumerate((14, 14, 15, 15)):
        at(u, logits, *groups[n], 1)
        at(u, finish2, *groups[n])
    for n, u in ((4, 16), (5, 18)):
        at(u, logits, *groups[n], 0)
        at(u, logits, *groups[n], 1)
        at(u, scores, *groups[n])
        at(u, finish2, *groups[n])
    for u in range(22):
        for fn, args in plan.get(u, []):
            fn(*args)

    def r1_send(s):
        to, n = (left, 2) if s == 0 else (right, 3)
        return rcopy(st.at[s], r1.at[n], r1_s.at[s], r1_r.at[n], to)

    def r1_far():
        return rcopy(st.at[1], r1.at[1], r1_s.at[1], r1_r.at[1], dev(0, 2, 0, 0))

    def join(parts):
        peak, hit = parts[0][0], parts[0][2]
        for t in parts[1:]:
            peak = jnp.maximum(peak, t[0])
            hit = jnp.maximum(hit, t[2])
        mass, hmass = None, None
        for t in parts:
            m = t[1] * jnp.exp(t[0] - peak)
            h = t[3] * jnp.exp(t[2] - hit)
            mass = m if mass is None else mass + m
            hmass = h if hmass is None else hmass + h
        return peak, mass, hit, hmass

    def r2_send(n):
        return rcopy(st2, r2.at[y], r2_s.at[n], r2_r.at[y], (d, (v + n) % 8))

    @pl.when(second)
    def _():
        for s in range(2):
            r1_send(s).start()

    @pl.when(first)
    def _():
        r1_far().start()
        r1[0] = st[0]
        for n in range(1, 4):
            rcopy(st.at[0], r1.at[n], r1_s.at[0], r1_r.at[n], right).wait_recv()

        for i, t in enumerate(join([[r1[n, i] for i in range(4)] for n in range(4)])):
            st2[i] = t
        for n in range(1, 8):
            r2_send(n).start()
        r2[y] = st2[...]

    for n in range(4):
        @pl.when(jnp.logical_not(first & (y == n)))
        def _():
            rcopy(st2, r2.at[n], r2_s.at[0], r2_r.at[n], dev(0, 0, 0, 1)).wait_recv()

    peak, mass, hit, hmass = join([[r2[n, i] for i in range(4)] for n in range(4)])
    loss = peak + jnp.log(mass) - hit - jnp.log(hmass)
    out[...] = loss[0:6]

    for ph in range(2):
        for e in range(1, 4):
            xe(ph, e).wait_send()
        for s in range(1, 5):
            for i in range(4):
                if s < 4 or i < 2:
                    zplus(ph, s, i).wait_send()
                if s < 4 or i >= 2:
                    zminus(ph, s, i).wait_send()
        for n in range(8):
            d2d(ph, z + d2d_z[n], n, c).wait_send()

    for o in range(2):
        keys_sent(o)

    @pl.when(first)
    def _():
        for n in range(3):
            mt_send(n).wait_send()
        for j in range(12):
            for s in range(2):
                hx_own(j, s).wait_send()

    def y_sent(s):
        for k in range(4):
            yown(s, k, True).wait_send()
            yown(s, k, False).wait_send()
            yfwd(s, k).wait_send()

    y_sent(1)

    @pl.when(second)
    def _():
        for j in range(12):
            hx_fwd(j).wait_send()
        y_sent(0)
        for s in range(2):
            r1_send(s).wait_send()

    @pl.when(first)
    def _():
        r1_far().wait_send()
        for n in range(1, 8):
            r2_send(n).wait_send()


def per_device(hidden, out_embed, key_proj, targets, doc_ids, list_owner, list_block, list_count):
    dma = pltpu.SemaphoreType.DMA
    loss = pl.pallas_call(
        kernel,
        out_shape=jax.ShapeDtypeStruct((6, 128), F32),
        in_specs=[pl.BlockSpec(memory_space=pltpu.HBM)] * 5 + [pl.BlockSpec(memory_space=pltpu.VMEM)] * 2 + [pl.BlockSpec(memory_space=pltpu.SMEM)],
        out_specs=pl.BlockSpec(memory_space=pltpu.VMEM),
        scratch_shapes=[
            pltpu.VMEM((3, 768, 4096), BF16),
            pltpu.VMEM((2, 2, 4096, 256), BF16),
            pltpu.VMEM((4096, 128), BF16),
            pltpu.VMEM((2, 768, 1024), F32),
            pltpu.VMEM((2, 768, 128), BF16),
            pltpu.VMEM((2, 16, 128), jnp.int32),
            pltpu.VMEM((3, 16, 128), jnp.int32),
            pltpu.VMEM((2, 512, 128), BF16),
            pltpu.VMEM((2, 8, 128), F32),
            pltpu.VMEM((2, 8, 128), F32),
            pltpu.VMEM((2, 8, 128), F32),
            pltpu.VMEM((2, 768, 128), F32),
            pltpu.VMEM((2, 4, 8, 128), F32),
            pltpu.VMEM((4, 4, 8, 128), F32),
            pltpu.VMEM((4, 8, 128), F32),
            pltpu.VMEM((4, 4, 8, 128), F32),
            dma((5,)),
            dma((2, 4)), dma((2, 4)),
            dma((2, 4, 4)), dma((2, 4, 4)), dma((2, 4, 4)), dma((2, 4, 4)),
            dma((2, 8)), dma((2, 8)),
            dma((2, 12)), dma((12,)), dma((2, 12)),
            dma((2, 4)), dma((2, 4)), dma((2, 4)), dma((2, 4)), dma((2, 4)), dma((2, 4)),
            dma((2, 2)), dma((2,)), dma((2, 2)), dma((2,)), dma((2,)), dma((2,)), dma((4,)), dma((2,)),
            dma((2,)), dma((4,)), dma((8,)), dma((4,)),
        ],
        compiler_params=pltpu.CompilerParams(
            collective_id=0, has_side_effects=True, vmem_limit_bytes=56 * 2**20
        ),
    )(hidden, out_embed, key_proj, targets, doc_ids, list_owner, list_block, list_count)
    return loss.reshape(768)


def solution(mesh):
    placed = (
        P("dp", None),
        P("dp", "vocab"),
        P(),
        P("dp"),
        P("dp"),
        P("dp", None),
        P("dp", None),
        P("dp"),
    )
    return jax.shard_map(per_device, mesh=mesh, in_specs=placed, out_specs=P("dp"), check_vma=False)
```

```python
import jax
import jax.numpy as jnp
from jax import lax
from jax.experimental import pallas as pl
from jax.experimental.pallas import tpu as pltpu
from jax.sharding import PartitionSpec as P

MESH = pl.DeviceIdType.MESH
NEG = -1e30
SCALE = 3.0 / 128**0.5
NX, NY, NZ = 4, 4, 8
CHUNK = 32
F32 = jnp.float32
WIDTH, OFFSET = (256, 256), (0, 256)
BF16 = jnp.bfloat16


def kernel(
    hid, emb, kproj, tgt, doc, lown, lblk, lcnt, out,
    hb, eb0, eb1, kp, kv, mt, om, kg, kt, kd, ko, tc, dc, sp, sm, st, last, rr, rl,
    loc_sem, xe_s, xe_r, z_s, z_r, dc_s, dc_r,
    hx_s, hf_s, hx_r, y_s, y_r, yf_r,
    kv_s, kv_r, om_s, om_r, kc_s, kc_r, mt_s, mt_r, r_s, r_r, rl_s, rl_r,
):
    d = lax.axis_index("dp")
    v = lax.axis_index("vocab")
    z, x = d // NX, d % NX
    y, c = v // 2, v % 2
    owner_here = z % NY == y
    first, second = c == 0, c == 1

    def eb(ph, row, rows, shard):
        w = WIDTH[ph]
        return (eb0, eb1)[ph].at[pl.ds(row, rows), pl.ds(pl.multiple_of(shard * w, 128), w)]

    def tok_x(s):
        return (x + 3 * c + 2 * s) % NX

    def dev(dz, dx, dy, dc):
        return (((z + dz) % NZ) * NX + (x + dx) % NX, ((y + dy) % NY) * 2 + (c + dc) % 2)

    def rcopy(src, dst, ssem, rsem, to):
        return pltpu.make_async_remote_copy(
            src_ref=src, dst_ref=dst, send_sem=ssem, recv_sem=rsem, device_id=to, device_id_type=MESH
        )

    bar = pltpu.get_barrier_semaphore()
    for to in [dev(1, 0, 0, 0), dev(NZ - 1, 0, 0, 0)] + [
        dev(0, 1, 0, 0), dev(0, 2, 0, 0), dev(0, 3, 0, 0), dev(0, 1, 0, 1), dev(0, 3, 0, 1)
    ]:
        pl.semaphore_signal(bar, inc=1, device_id=to, device_id_type=MESH)
    for n in range(1, 8):
        pl.semaphore_signal(bar, inc=1, device_id=(d, (v + n) % 8), device_id_type=MESH)

    om_loads = []
    for n in range(6):
        om_loads.append(pltpu.make_async_copy(tgt.at[pl.ds(n * 128, 128)], om.at[2, n], loc_sem.at[4]))
        om_loads.append(pltpu.make_async_copy(doc.at[pl.ds(n * 128, 128)], om.at[2, 6 + n], loc_sem.at[4]))
    for cp in om_loads:
        cp.start()
    emb_loads = []
    for ph in range(2):
        col = pl.multiple_of(x * 512 + OFFSET[ph], 128)
        cp = pltpu.make_async_copy(
            emb.at[:, pl.ds(col, WIDTH[ph])], eb(ph, pl.multiple_of(d * 128, 128), 128, c), loc_sem.at[2 + ph]
        )
        cp.start()
        emb_loads.append(cp)
    own_slot = 2 * c
    kp_load = pltpu.make_async_copy(kproj, kp, loc_sem.at[1])
    kp_load.start()
    hid_load = pltpu.make_async_copy(hid, hb.at[own_slot], loc_sem.at[0])
    hid_load.start()
    om[2, 12:16] = jnp.zeros((4, 128), jnp.int32)
    om[2, 12:13, 0:64] = lown[...]
    om[2, 13:14, 0:64] = lblk[...]
    om[2, 14:15] = jnp.full((1, 128), lcnt[0], jnp.int32)
    pl.semaphore_wait(bar, 14)

    def eslot(ph, zz, i):
        row = ((zz % NZ) * NX + (x + i) % NX) * 128
        return eb(ph, pl.multiple_of(row, 128), 128, c)

    def xe(ph, e):
        col = pl.multiple_of(((x + e) % NX) * 512 + OFFSET[ph], 128)
        return rcopy(
            emb.at[:, pl.ds(col, WIDTH[ph])],
            eb(ph, pl.multiple_of(d * 128, 128), 128, c),
            xe_s.at[0], xe_r.at[ph, 4 - e], dev(0, e, 0, 0),
        )

    def xe_in(ph, i):
        return rcopy(
            emb.at[:, pl.ds(0, WIDTH[ph])], eslot(ph, z, i), xe_s.at[0], xe_r.at[ph, i], dev(0, i, 0, 0)
        )

    def zplus(ph, s, i):
        ref = eslot(ph, z - (s - 1) + NZ, i)
        return rcopy(ref, ref, z_s.at[0], z_r.at[ph, s - 1, i], dev(1, 0, 0, 0))

    def zminus(ph, s, i):
        ref = eslot(ph, z + (s - 1), i)
        return rcopy(ref, ref, z_s.at[0], z_r.at[ph, s - 1, i - 2 if s == 4 else i], dev(NZ - 1, 0, 0, 0))

    def z_in(ph, s, i):
        ref = eb(ph, 0, 256, c)
        return rcopy(ref, ref, z_s.at[0], z_r.at[ph, s - 1, i], dev(1, 0, 0, 0))

    def d2d(ph, zz, n, shard):
        ref = eb(ph, pl.multiple_of((zz % NZ) * 512, 512), 512, shard)
        return rcopy(ref, ref, dc_s.at[0], dc_r.at[ph], dev(0, 0, 0, 1))

    d2d_z = [0, 7, 6, 5, 1, 2, 3, 4]

    def z_first(ph, pair):
        for i in ((0,), (1,), (2, 3))[pair]:
            if i == 0:
                emb_loads[ph].wait()
            else:
                xe_in(ph, i).wait_recv()
            zplus(ph, 1, i).start()
            zminus(ph, 1, i).start()
        if pair == 2:
            d2d(ph, z, 0, c).start()

    def z_event(ph, s, pair):
        if s < 4:
            for i in (0, 1) if pair == 0 else (2, 3):
                z_in(ph, s, i).wait_recv()
                if s < 3 or i < 2:
                    zplus(ph, s + 1, i).start()
                if s < 3 or i >= 2:
                    zminus(ph, s + 1, i).start()
            if pair == 1:
                d2d(ph, z + NZ - s, s, c).start()
                d2d(ph, z + s, 3 + s, c).start()
        else:
            for i in (0, 1):
                z_in(ph, 4, i).wait_recv()
            d2d(ph, z + 4, 7, c).start()

    def embed_ready(ph):
        ref = eb(ph, 0, 4096, 1 - c)
        rcopy(ref, ref, dc_s.at[0], dc_r.at[ph], dev(0, 0, 0, 1)).wait_recv()

    def rows_of(j, yy):
        b, k = j // 4, j % 4
        if b == 0:
            return pl.ds(pl.multiple_of(256 + (yy % NY) * 128 + k * CHUNK, CHUNK), CHUNK)
        return pl.ds((b - 1) * 128 + k * CHUNK, CHUNK)

    right, left = dev(0, 1, 0, 1), dev(0, 3, 0, 1)

    def hx_own(j, s):
        r = rows_of(j, y)
        return rcopy(hid.at[r], hb.at[s, r], hx_s.at[0], hx_r.at[j], (right, left)[s])

    def hx_fwd(j):
        r = rows_of(j, y)
        s = 0 if j % 4 < 2 else 1
        return rcopy(hb.at[s, r], hb.at[1, r], hf_s.at[0], hx_r.at[j], (right, left)[s])

    def arrived(sem, rows):
        ref = hb.at[0, pl.ds(0, rows)]
        rcopy(ref, ref, hf_s.at[0], sem, right).wait_recv()

    def yown(s, k, up):
        r = rows_of(k, y)
        if up:
            return rcopy(hb.at[s, r], hb.at[s, r], y_s.at[0], y_r.at[k], dev(0, 0, 1, 0))
        return rcopy(hb.at[s, r], hb.at[s, r], y_s.at[0], y_r.at[k], dev(0, 0, 3, 0))

    def yfwd(s, k):
        if k < 2:
            r = rows_of(k, y + 3)
            return rcopy(hb.at[s, r], hb.at[s, r], y_s.at[0], yf_r.at[k], dev(0, 0, 1, 0))
        r = rows_of(k, y + 1)
        return rcopy(hb.at[s, r], hb.at[s, r], y_s.at[0], yf_r.at[k], dev(0, 0, 3, 0))

    def x_send(j):
        @pl.when(first)
        def _():
            hx_own(j, 0).start()
            hx_own(j, 1).start()

    def x_near(j):
        @pl.when(second)
        def _():
            arrived(hx_r.at[j], 64)
            if j < 4:
                hx_fwd(j).start()
                for s in range(2):
                    yown(s, j, True).start()
                    yown(s, j, False).start()

    def x_forward(*js):
        @pl.when(second)
        def _():
            for j in js:
                hx_fwd(j).start()

    def x_far(*js):
        @pl.when(first)
        def _():
            for j in js:
                arrived(hx_r.at[j], 32)
                if j < 4:
                    yown(1, j, True).start()
                    yown(1, j, False).start()

    def y_near(k):
        @pl.when(second)
        def _():
            arrived(y_r.at[k], 128)
            yfwd(0, k).start()
            yfwd(1, k).start()

    def y_far(k):
        @pl.when(first)
        def _():
            arrived(y_r.at[k], 64)
            yfwd(1, k).start()

    def y_last(k):
        @pl.when(first)
        def _():
            arrived(yf_r.at[k], 32)

        @pl.when(second)
        def _():
            arrived(yf_r.at[k], 64)

    my_owner = z // NY
    half = pl.ds(pl.multiple_of(c * 384, 384), 384)
    up, down = dev(1, 0, 0, 0), dev(NZ - 1, 0, 0, 0)

    def key_copy(o, n, to):
        return rcopy(kv.at[o, half], kv.at[o, half], kv_s.at[o], kv_r.at[o], to)

    def int_copy(o, n, to):
        return rcopy(om.at[o], om.at[o], om_s.at[o], om_r.at[o], to)

    def key_cross(o):
        return rcopy(kv.at[o, half], kv.at[o, half], kc_s.at[0], kc_r.at[o], dev(0, 0, 0, 1))

    def key_cross_in(o):
        ref = kv.at[o, pl.ds(pl.multiple_of(384 - c * 384, 384), 384)]
        return rcopy(ref, ref, kc_s.at[0], kc_r.at[o], dev(0, 0, 0, 1))

    def mt_send(n):
        to, s = ((dev(0, 2, 0, 0), 1), (right, 0), (left, 1))[n]
        return rcopy(om.at[2], mt.at[s], mt_s.at[0], mt_r.at[s], to)

    def small_sends():
        for cp in om_loads:
            cp.wait()

        @pl.when(first)
        def _():
            for n in range(3):
                mt_send(n).start()
            mt[0] = om[2]

    def key_sends():
        hid_load.wait()
        kp_load.wait()

        @pl.when(owner_here)
        def _():
            kv[my_owner, half, :] = jnp.dot(
                hb[own_slot, half, :], kp[...], preferred_element_type=F32
            ).astype(BF16)
            om[my_owner] = om[2]
            key_cross(my_owner).start()
            for n, to in enumerate((up, down)):
                key_copy(my_owner, n, to).start()
                int_copy(my_owner, n, to).start()

    def hops(o):
        return (z - y - NY * o + 2 * NZ) % NZ

    def key_relay(hop):
        for o in range(2):
            key_relay_of(o, hop)

    def key_relay_of(o, hop):
        @pl.when((hops(o) == hop) | ((hops(o) == NZ - hop) & (hop < 4)))
        def _():
            key_copy(o, 0, up).wait_recv()
            int_copy(o, 0, up).wait_recv()
            key_cross(o).start()

        if hop < 4:
            @pl.when(hops(o) == hop)
            def _():
                key_copy(o, 0, up).start()
                int_copy(o, 0, up).start()

        if hop < 3:
            @pl.when(hops(o) == NZ - hop)
            def _():
                key_copy(o, 1, down).start()
                int_copy(o, 1, down).start()

    def keys_sent(o):
        def sent(ref, sem):
            rcopy(ref, ref, sem, kv_r.at[o], up).wait_send()

        @pl.when(hops(o) == 0)
        def _():
            sent(kv.at[o], kv_s.at[o])
            sent(om.at[0:2], om_s.at[o])

        @pl.when(((hops(o) > 0) & (hops(o) < 4)) | (hops(o) > 5))
        def _():
            sent(kv.at[o, half], kv_s.at[o])
            sent(om.at[o], om_s.at[o])

    def keys_ready():
        for o in range(2):
            key_cross_in(o).wait_recv()

    def tokens_ready():
        rcopy(om.at[2], mt.at[1], mt_s.at[0], mt_r.at[1], right).wait_recv()

        @pl.when(second)
        def _():
            rcopy(om.at[2], mt.at[0], mt_s.at[0], mt_r.at[0], right).wait_recv()

        def turn(blk, _):
            for s in range(2):
                tc[s, blk] = column(s, blk)
                dc[s, blk] = column(s, 6 + blk)
            return 0

        lax.fori_loop(0, 6, turn, 0)

    def memory_ready():
        keys_ready()
        lane = lax.broadcasted_iota(jnp.int32, (1, 128), 1)
        for s in range(2):
            live = lane < mt[s, 14:15, :]
            for o in range(2):
                owner_id = (y + NY * o) * NX + x
                named = live & (mt[s, 12:13, :] == owner_id)
                blocks = mt[s, 13:14, :].astype(F32)
                most = jnp.max(jnp.where(named, blocks, -1.0), axis=1, keepdims=True)
                least = jnp.min(jnp.where(named, blocks, 99.0), axis=1, keepdims=True)
                least = jnp.where(least == most, 99.0, least)
                mine = jnp.where(owner_id == z * NX + tok_x(s), 1.0, 0.0)
                for k, at_block in enumerate((most, least)):
                    n = 2 * o + k
                    keys = jnp.zeros((128, 128), F32)
                    tgts, docs = jnp.zeros((1, 128), F32), jnp.full((1, 128), -1.0, F32)
                    for b in range(6):
                        w = jnp.where(at_block == float(b), 1.0, 0.0)
                        keys = keys + w * kv[o, b * 128 : b * 128 + 128, :].astype(F32)
                        tgts = tgts + w * om[o, b : b + 1, :].astype(F32)
                        docs = docs + w * (om[o, 6 + b : 7 + b, :].astype(F32) + 1.0)
                    kg[s, n * 128 : n * 128 + 128, :] = keys.astype(BF16)
                    kt[s, n : n + 1, :] = tgts
                    kd[s, n : n + 1, :] = docs
                    ko[s, n : n + 1, :] = jnp.broadcast_to(mine * (at_block + 1.0) - 1.0, (1, 128))

    def column(s, row):
        return jnp.broadcast_to(mt[s, pl.ds(row, 1), :].astype(F32), (128, 128)).T

    def rows_at(blk):
        return pl.ds(pl.multiple_of(blk * 128, 128), 128)

    def two_blocks(sa, ba, sb, bb):
        return jnp.concatenate([hb[sa, rows_at(ba), :], hb[sb, rows_at(bb), :]], axis=0)

    def peaks(tiles):
        top = tiles[0]
        for t in tiles[1:]:
            top = jnp.maximum(top, t)
        top = jnp.max(top, axis=1, keepdims=True)
        total = jnp.exp(tiles[0] - top)
        for t in tiles[1:]:
            total = total + jnp.exp(t - top)
        return top, jnp.sum(total, axis=1, keepdims=True)

    def halves(n):
        sa, ba, sb, bb = groups[n]
        return (0, sa, ba), (1, sb, bb)

    def lane_tile(first_lane, columns):
        i1 = lax.broadcasted_iota(jnp.int32, (128, 128), 1)
        t = columns[-1]
        for k in range(len(columns) - 2, -1, -1):
            t = jnp.where(i1 == first_lane + k, columns[k], t)
        return t

    def score_tiles(n):
        q2 = jnp.dot(two_blocks(*groups[n]), kp[...], preferred_element_type=F32).astype(BF16)
        i0 = lax.broadcasted_iota(jnp.int32, (128, 128), 0)
        i1 = lax.broadcasted_iota(jnp.int32, (128, 128), 1)
        eye = i0 == i1
        out_tiles = []
        for h, s, blk in halves(n):
            q = q2[h * 128 : h * 128 + 128]
            tcol, dcol = tc[s, blk], dc[s, blk]
            sc = SCALE * lax.dot_general(q, kg[s], (((1,), (1,)), ((), ())), preferred_element_type=F32)
            kept, hits = [], []
            for m in range(4):
                mine = jnp.where(ko[s, m : m + 1, :] == blk.astype(F32), 2.0, 0.0)
                keep = kd[s, m : m + 1, :] == dcol + jnp.where(eye, mine, 0.0)
                sk = jnp.where(keep, sc[:, m * 128 : m * 128 + 128], NEG)
                kept.append(sk)
                hits.append(jnp.where(kt[s, m : m + 1, :] == tcol, sk, NEG))
            out_tiles.append(lane_tile(4, [*peaks(kept), *peaks(hits)]))
        return out_tiles

    def logit_columns(n, phs):
        a = two_blocks(*groups[n])
        lane = lax.broadcasted_iota(jnp.int32, (1, 128), 1)
        res = [
            (ph, cs, jnp.dot(a, (eb0, eb1)[ph][:, cs * 256 : cs * 256 + 256], preferred_element_type=F32))
            for ph in phs
            for cs in range(2)
        ]
        out_columns = []
        for h, s, blk in halves(n):
            tcol = tc[s, blk]
            tiles, pick = [], None
            for ph, cs, r in res:
                for k in range(2):
                    t = r[h * 128 : h * 128 + 128, k * 128 : k * 128 + 128]
                    base = (2 * y + cs) * 2048 + x * 512 + OFFSET[ph] + k * 128
                    hit = jnp.where((lane + base).astype(F32) == tcol, t, NEG)
                    pick = hit if pick is None else jnp.maximum(pick, hit)
                    tiles.append(t)
            out_columns.append([*peaks(tiles), jnp.max(pick, axis=1, keepdims=True)])
        return out_columns

    def early(n):
        columns = logit_columns(n, (0,))
        memory = score_tiles(n)
        for h in range(2):
            sp[n, h] = lane_tile(8, columns[h])
            sm[n, h] = memory[h]

    def late(was_early, *ns):
        rows = [r for n in ns for r in late_rows(n, was_early)]
        for n, h, s, blk, values in rows:
            for k, row in enumerate(values):
                if n < 5:
                    st[s, k, pl.ds(blk, 1), :] = row
                else:
                    last[s, pl.ds(k + (4 * (1 - c) if h else 0), 1), :] = row

    def late_rows(n, was_early):
        i1 = lax.broadcasted_iota(jnp.int32, (128, 128), 1)
        columns = logit_columns(n, (1,) if was_early else (0, 1))
        memory = [sm[n, 0], sm[n, 1]] if was_early else score_tiles(n)
        rows = []
        for h, s, blk in halves(n):
            t = jnp.where(i1 < 4, lane_tile(0, columns[h]), memory[h])
            if was_early:
                t = jnp.where(i1 < 8, t, sp[n, h])
            t = t.T
            parts = [(t[0:1], t[1:2], t[2:3], 1.0), (t[4:5], t[5:6], t[6:7], t[7:8])]
            if was_early:
                parts.append((t[8:9], t[9:10], t[10:11], 1.0))
            peak, hit = parts[0][0], parts[0][2]
            for lp, _, lh, _ in parts[1:]:
                peak, hit = jnp.maximum(peak, lp), jnp.maximum(hit, lh)
            mass, hmass = None, None
            for lp, lm, lh, hm in parts:
                m, g = lm * jnp.exp(lp - peak), hm * jnp.exp(lh - hit)
                mass = m if mass is None else mass + m
                hmass = g if hmass is None else hmass + g
            rows.append((n, h, s, blk, (peak, mass, hit, hmass)))
        return rows

    def st_send(s, n):
        to = (z * NX + tok_x(s), (v + n) % 8)
        return rcopy(st.at[s], rr.at[(2 * c + s) * NY + y], r_s.at[0], r_r.at[0], to)

    def last_send(s, n):
        to = (z * NX + tok_x(s), (v + n) % 8)
        return rcopy(last.at[s], rl.at[(2 * c + s) * NY + y - 4], rl_s.at[0], rl_r.at[0], to)

    def most_results():
        for n in range(1, 8):
            for s in range(2):
                st_send(s, n).start()
        st_send(1, 0).start()

        @pl.when(second)
        def _():
            st_send(0, 0).start()

        @pl.when(first)
        def _():
            rr[y] = st[0]

    for e in range(1, 4):
        xe(0, e).start()
    z_first(0, 0)
    z_first(1, 0)
    x_send(0)
    x_send(1)
    for e in range(1, 4):
        xe(1, e).start()
    small_sends()
    for j in range(2, 12):
        x_send(j)
    key_sends()
    z_first(0, 1)
    z_first(0, 2)

    z_events = [(ph, s, q) for ph in range(2) for s in range(1, 5) for q in range(2 if s < 4 else 1)]
    qy, qd, qu, qo = 2 + y, 2 + (y + 3) % 4, 2 + (y + 1) % 4, 2 + (y + 2) % 4
    plan = {}

    def at(u, fn, *args):
        plan.setdefault(u, []).append((fn, args))

    for n, ev in enumerate(z_events):
        at(n, z_event, *ev)
    for hop, u in ((1, 0), (2, 2), (3, 4), (4, 5)):
        at(u, key_relay, hop)
    at(3, z_first, 1, 1)
    at(4, z_first, 1, 2)
    for j, u in enumerate((-1, 1, 4, 5, 7, 8, 9, 10, 11, 12, 14, 14)):
        at(u, x_near, j)
    for u, js in ((11, (4, 6)), (12, (5, 7)), (14, (8, 10)), (14, (9, 11))):
        at(u, x_forward, *js)
    for u, js in ((4, (0,)), (5, (1,)), (7, (2,)), (8, (3,)), (15, (4, 6)), (16, (5, 7)), (17, (8, 10)), (18, (9, 11))):
        at(u, x_far, *js)
    for k in range(4):
        at((6, 8, 10, 12)[k], y_near, k)
        at((10, 11, 13, 14)[k], y_far, k)
        at((15, 17, 16, 18)[k], y_last, k)
    groups = [
        [jnp.where(first, a, b) for a, b in zip(on_first, on_second)]
        for on_first, on_second in (
            ((0, 0, 0, 1), (0, qy, 1, qy)),
            ((0, qy, 0, qd), (0, 0, 1, 0)),
            ((0, qu, 0, qo), (0, qd, 1, qd)),
            ((1, qd, 1, qu), (0, qu, 1, qu)),
            ((1, qy, 1, 0), (0, 1, 1, 1)),
            ((1, 1, 1, qo), (0, qo, 1, qo)),
        )
    ]
    at(4, tokens_ready)
    at(7, memory_ready)
    at(8, embed_ready, 0)
    at(8, early, 0)
    at(10, early, 1)
    at(12, early, 2)
    at(14, early, 3)
    at(14, embed_ready, 1)
    at(14, late, True, 0, 1)
    at(14, late, True, 2, 3)
    at(16, late, False, 4)
    at(18, late, False, 5)
    at(17, most_results)
    for u in range(-1, 22):
        for fn, args in plan.get(u, []):
            fn(*args)

    for n in range(8):
        last_send(1, n).start()

    @pl.when(second)
    def _():
        for n in range(8):
            last_send(0, n).start()

    @pl.when(first)
    def _():
        rcopy(rr.at[0:15], rr.at[0:15], r_s.at[0], r_r.at[0], right).wait_recv()

    @pl.when(second)
    def _():
        rcopy(rr, rr, r_s.at[0], r_r.at[0], right).wait_recv()

    rcopy(rl, rl, rl_s.at[0], rl_r.at[0], right).wait_recv()
    for n in range(4):
        far_blk = 2 + (n + 2) % 4
        for k in range(4):
            rr[4 + n, k, 1:2] = rl[n, k : k + 1]
            rr[4 + n, k, far_blk : far_blk + 1] = rl[n, 4 + k : 5 + k]
            for m in (4, 8):
                rr[4 + m + n, k, far_blk : far_blk + 1] = rl[m + n, k : k + 1]

    peak, hit = rr[0, 0], rr[0, 2]
    for n in range(1, 16):
        peak = jnp.maximum(peak, rr[n, 0])
        hit = jnp.maximum(hit, rr[n, 2])
    mass = rr[0, 1] * jnp.exp(rr[0, 0] - peak)
    hmass = rr[0, 3] * jnp.exp(rr[0, 2] - hit)
    for n in range(1, 16):
        mass = mass + rr[n, 1] * jnp.exp(rr[n, 0] - peak)
        hmass = hmass + rr[n, 3] * jnp.exp(rr[n, 2] - hit)
    loss = peak + jnp.log(mass) - hit - jnp.log(hmass)
    out[...] = loss[0:6]

    def sent(ref, sem):
        rcopy(ref, ref, sem.at[0], dc_r.at[0], right).wait_send()

    sent(hb.at[0, pl.ds(0, 48)], xe_s)
    sent(hb.at[0, pl.ds(0, 448)], z_s)
    sent(hb.at[0, pl.ds(0, 512)], dc_s)
    sent(kv.at[0], kc_s)
    for o in range(2):
        keys_sent(o)

    @pl.when(first)
    def _():
        sent(om, mt_s)
        sent(hb.at[0], hx_s)
        sent(hb.at[0, pl.ds(0, 384)], y_s)
        sent(rr.at[0:15], r_s)
        sent(rl.at[0:8], rl_s)

    @pl.when(second)
    def _():
        sent(hb.at[0, pl.ds(0, 384)], hf_s)
        sent(hb.at[0], y_s)
        sent(rr, r_s)
        sent(tc.at[0, 0:1], rl_s)


def per_device(hidden, out_embed, key_proj, targets, doc_ids, list_owner, list_block, list_count):
    dma = pltpu.SemaphoreType.DMA
    loss = pl.pallas_call(
        kernel,
        out_shape=jax.ShapeDtypeStruct((6, 128), F32),
        in_specs=[pl.BlockSpec(memory_space=pltpu.HBM)] * 5 + [pl.BlockSpec(memory_space=pltpu.VMEM)] * 2 + [pl.BlockSpec(memory_space=pltpu.SMEM)],
        out_specs=pl.BlockSpec(memory_space=pltpu.VMEM),
        scratch_shapes=[
            pltpu.VMEM((3, 768, 4096), BF16),
            pltpu.VMEM((4096, 512), BF16),
            pltpu.VMEM((4096, 512), BF16),
            pltpu.VMEM((4096, 128), BF16),
            pltpu.VMEM((2, 768, 128), BF16),
            pltpu.VMEM((2, 16, 128), jnp.int32),
            pltpu.VMEM((3, 16, 128), jnp.int32),
            pltpu.VMEM((2, 512, 128), BF16),
            pltpu.VMEM((2, 8, 128), F32),
            pltpu.VMEM((2, 8, 128), F32),
            pltpu.VMEM((2, 8, 128), F32),
            pltpu.VMEM((2, 6, 128, 128), F32),
            pltpu.VMEM((2, 6, 128, 128), F32),
            pltpu.VMEM((4, 2, 128, 128), F32),
            pltpu.VMEM((4, 2, 128, 128), F32),
            pltpu.VMEM((2, 4, 8, 128), F32),
            pltpu.VMEM((2, 8, 128), F32),
            pltpu.VMEM((16, 4, 8, 128), F32),
            pltpu.VMEM((12, 8, 128), F32),
            dma((5,)),
            dma((1,)), dma((2, 4)), dma((1,)), dma((2, 4, 4)), dma((1,)), dma((2,)),
            dma((1,)), dma((1,)), dma((12,)), dma((1,)), dma((4,)), dma((4,)),
            dma((2,)), dma((2,)), dma((2,)), dma((2,)), dma((1,)), dma((2,)), dma((1,)), dma((2,)),
            dma((1,)), dma((1,)), dma((1,)), dma((1,)),
        ],
        compiler_params=pltpu.CompilerParams(
            collective_id=0, has_side_effects=True, vmem_limit_bytes=56 * 2**20
        ),
    )(hidden, out_embed, key_proj, targets, doc_ids, list_owner, list_block, list_count)
    return loss.reshape(768)


def solution(mesh):
    placed = (
        P("dp", None),
        P("dp", "vocab"),
        P(),
        P("dp"),
        P("dp"),
        P("dp", None),
        P("dp", None),
        P("dp"),
    )
    return jax.shard_map(per_device, mesh=mesh, in_specs=placed, out_specs=P("dp"), check_vma=False)
```

```python
import jax
import jax.numpy as jnp
from jax import lax
from jax.experimental import pallas as pl
from jax.experimental.pallas import tpu as pltpu
from jax.sharding import PartitionSpec as P

MESH = pl.DeviceIdType.MESH
NEG = -1e30
SCALE = 3.0 / 128**0.5
NX, NY, NZ = 4, 4, 8
CHUNK = 32
F32 = jnp.float32
WIDTH, OFFSET = (256, 256), (0, 256)
BF16 = jnp.bfloat16


def kernel(
    hid, emb, kproj, tgt, doc, lown, lblk, lcnt, out,
    hb, eb0, eb1, kp, kv, mt, om, kg, kt, kd, ko, tc, dc, sp, sm, st, last, rr, rl,
    loc_sem, xe_s, xe_r, z_s, z_r, dc_s, dc_r,
    hx_s, hf_s, hx_r, y_s, y_r, yf_r,
    kv_s, kv_r, om_s, om_r, kc_s, kc_r, mt_s, mt_r, r_s, r_r, rl_s, rl_r,
):
    d = lax.axis_index("dp")
    v = lax.axis_index("vocab")
    z, x = d // NX, d % NX
    y, c = v // 2, v % 2
    owner_here = z % NY == y
    first, second = c == 0, c == 1

    def eb(ph, row, rows, shard):
        w = WIDTH[ph]
        return (eb0, eb1)[ph].at[pl.ds(row, rows), pl.ds(pl.multiple_of(shard * w, 128), w)]

    def tok_x(s):
        return (x + 3 * c + 2 * s) % NX

    def dev(dz, dx, dy, dc):
        return (((z + dz) % NZ) * NX + (x + dx) % NX, ((y + dy) % NY) * 2 + (c + dc) % 2)

    def rcopy(src, dst, ssem, rsem, to):
        return pltpu.make_async_remote_copy(
            src_ref=src, dst_ref=dst, send_sem=ssem, recv_sem=rsem, device_id=to, device_id_type=MESH
        )

    bar = pltpu.get_barrier_semaphore()
    for to in [dev(1, 0, 0, 0), dev(NZ - 1, 0, 0, 0)] + [
        dev(0, 1, 0, 0), dev(0, 2, 0, 0), dev(0, 3, 0, 0), dev(0, 1, 0, 1), dev(0, 3, 0, 1)
    ]:
        pl.semaphore_signal(bar, inc=1, device_id=to, device_id_type=MESH)
    for n in range(1, 8):
        pl.semaphore_signal(bar, inc=1, device_id=(d, (v + n) % 8), device_id_type=MESH)

    om_loads = []
    for n in range(6):
        om_loads.append(pltpu.make_async_copy(tgt.at[pl.ds(n * 128, 128)], om.at[2, n], loc_sem.at[4]))
        om_loads.append(pltpu.make_async_copy(doc.at[pl.ds(n * 128, 128)], om.at[2, 6 + n], loc_sem.at[4]))
    for cp in om_loads:
        cp.start()
    emb_loads = []
    for ph in range(2):
        col = pl.multiple_of(x * 512 + OFFSET[ph], 128)
        cp = pltpu.make_async_copy(
            emb.at[:, pl.ds(col, WIDTH[ph])], eb(ph, pl.multiple_of(d * 128, 128), 128, c), loc_sem.at[2 + ph]
        )
        cp.start()
        emb_loads.append(cp)
    own_slot = 2 * c
    kp_load = pltpu.make_async_copy(kproj, kp, loc_sem.at[1])
    kp_load.start()
    hid_load = pltpu.make_async_copy(hid, hb.at[own_slot], loc_sem.at[0])
    hid_load.start()
    om[2, 12:16] = jnp.zeros((4, 128), jnp.int32)
    om[2, 12:13, 0:64] = lown[...]
    om[2, 13:14, 0:64] = lblk[...]
    om[2, 14:15] = jnp.full((1, 128), lcnt[0], jnp.int32)
    pl.semaphore_wait(bar, 14)

    def eslot(ph, zz, i):
        row = ((zz % NZ) * NX + (x + i) % NX) * 128
        return eb(ph, pl.multiple_of(row, 128), 128, c)

    def xe(ph, e):
        col = pl.multiple_of(((x + e) % NX) * 512 + OFFSET[ph], 128)
        return rcopy(
            emb.at[:, pl.ds(col, WIDTH[ph])],
            eb(ph, pl.multiple_of(d * 128, 128), 128, c),
            xe_s.at[0], xe_r.at[ph, 4 - e], dev(0, e, 0, 0),
        )

    def xe_in(ph, i):
        return rcopy(
            emb.at[:, pl.ds(0, WIDTH[ph])], eslot(ph, z, i), xe_s.at[0], xe_r.at[ph, i], dev(0, i, 0, 0)
        )

    def zplus(ph, s, i):
        ref = eslot(ph, z - (s - 1) + NZ, i)
        return rcopy(ref, ref, z_s.at[0], z_r.at[ph, s - 1, i], dev(1, 0, 0, 0))

    def zminus(ph, s, i):
        ref = eslot(ph, z + (s - 1), i)
        return rcopy(ref, ref, z_s.at[0], z_r.at[ph, s - 1, i - 2 if s == 4 else i], dev(NZ - 1, 0, 0, 0))

    def z_in(ph, s, i):
        ref = eb(ph, 0, 256, c)
        return rcopy(ref, ref, z_s.at[0], z_r.at[ph, s - 1, i], dev(1, 0, 0, 0))

    def d2d(ph, zz, n, shard):
        ref = eb(ph, pl.multiple_of((zz % NZ) * 512, 512), 512, shard)
        return rcopy(ref, ref, dc_s.at[0], dc_r.at[ph], dev(0, 0, 0, 1))

    d2d_z = [0, 7, 6, 5, 1, 2, 3, 4]

    def z_first(ph, pair):
        for i in ((0,), (1,), (2, 3))[pair]:
            if i == 0:
                emb_loads[ph].wait()
            else:
                xe_in(ph, i).wait_recv()
            zplus(ph, 1, i).start()
            zminus(ph, 1, i).start()
        if pair == 2:
            d2d(ph, z, 0, c).start()

    def z_event(ph, s, pair):
        if s < 4:
            for i in (0, 1) if pair == 0 else (2, 3):
                z_in(ph, s, i).wait_recv()
                if s < 3 or i < 2:
                    zplus(ph, s + 1, i).start()
                if s < 3 or i >= 2:
                    zminus(ph, s + 1, i).start()
            if pair == 1:
                d2d(ph, z + NZ - s, s, c).start()
                d2d(ph, z + s, 3 + s, c).start()
        else:
            for i in (0, 1):
                z_in(ph, 4, i).wait_recv()
            d2d(ph, z + 4, 7, c).start()

    def embed_ready(ph):
        ref = eb(ph, 0, 4096, 1 - c)
        rcopy(ref, ref, dc_s.at[0], dc_r.at[ph], dev(0, 0, 0, 1)).wait_recv()

    def rows_of(j, yy):
        b, k = j // 4, j % 4
        if b == 0:
            return pl.ds(pl.multiple_of(256 + (yy % NY) * 128 + k * CHUNK, CHUNK), CHUNK)
        return pl.ds((b - 1) * 128 + k * CHUNK, CHUNK)

    right, left = dev(0, 1, 0, 1), dev(0, 3, 0, 1)

    def hx_own(j, s):
        r = rows_of(j, y)
        return rcopy(hid.at[r], hb.at[s, r], hx_s.at[0], hx_r.at[j], (right, left)[s])

    def hx_fwd(j):
        r = rows_of(j, y)
        s = 0 if j % 4 < 2 else 1
        return rcopy(hb.at[s, r], hb.at[1, r], hf_s.at[0], hx_r.at[j], (right, left)[s])

    def arrived(sem, rows):
        ref = hb.at[0, pl.ds(0, rows)]
        rcopy(ref, ref, hf_s.at[0], sem, right).wait_recv()

    def yown(s, k, up):
        r = rows_of(k, y)
        if up:
            return rcopy(hb.at[s, r], hb.at[s, r], y_s.at[0], y_r.at[k], dev(0, 0, 1, 0))
        return rcopy(hb.at[s, r], hb.at[s, r], y_s.at[0], y_r.at[k], dev(0, 0, 3, 0))

    def yfwd(s, k):
        if k < 2:
            r = rows_of(k, y + 3)
            return rcopy(hb.at[s, r], hb.at[s, r], y_s.at[0], yf_r.at[k], dev(0, 0, 1, 0))
        r = rows_of(k, y + 1)
        return rcopy(hb.at[s, r], hb.at[s, r], y_s.at[0], yf_r.at[k], dev(0, 0, 3, 0))

    def x_send(j):
        @pl.when(first)
        def _():
            hx_own(j, 0).start()
            hx_own(j, 1).start()

    def x_near(j):
        @pl.when(second)
        def _():
            arrived(hx_r.at[j], 64)
            if j < 4:
                hx_fwd(j).start()
                for s in range(2):
                    yown(s, j, True).start()
                    yown(s, j, False).start()

    def x_forward(*js):
        @pl.when(second)
        def _():
            for j in js:
                hx_fwd(j).start()

    def x_far(*js):
        @pl.when(first)
        def _():
            for j in js:
                arrived(hx_r.at[j], 32)
                if j < 4:
                    yown(1, j, True).start()
                    yown(1, j, False).start()

    def y_near(k):
        @pl.when(second)
        def _():
            arrived(y_r.at[k], 128)
            yfwd(0, k).start()
            yfwd(1, k).start()

    def y_far(k):
        @pl.when(first)
        def _():
            arrived(y_r.at[k], 64)
            yfwd(1, k).start()

    def y_last(k):
        @pl.when(first)
        def _():
            arrived(yf_r.at[k], 32)

        @pl.when(second)
        def _():
            arrived(yf_r.at[k], 64)

    my_owner = z // NY
    half = pl.ds(pl.multiple_of(c * 384, 384), 384)
    up, down = dev(1, 0, 0, 0), dev(NZ - 1, 0, 0, 0)

    def key_copy(o, n, to):
        return rcopy(kv.at[o, half], kv.at[o, half], kv_s.at[o], kv_r.at[o], to)

    def int_copy(o, n, to):
        return rcopy(om.at[o], om.at[o], om_s.at[o], om_r.at[o], to)

    def key_cross(o):
        return rcopy(kv.at[o, half], kv.at[o, half], kc_s.at[0], kc_r.at[o], dev(0, 0, 0, 1))

    def key_cross_in(o):
        ref = kv.at[o, pl.ds(pl.multiple_of(384 - c * 384, 384), 384)]
        return rcopy(ref, ref, kc_s.at[0], kc_r.at[o], dev(0, 0, 0, 1))

    def mt_send(n):
        to, s = ((dev(0, 2, 0, 0), 1), (right, 0), (left, 1))[n]
        return rcopy(om.at[2], mt.at[s], mt_s.at[0], mt_r.at[s], to)

    def small_sends():
        for cp in om_loads:
            cp.wait()

        @pl.when(first)
        def _():
            for n in range(3):
                mt_send(n).start()
            mt[0] = om[2]

    def key_sends():
        hid_load.wait()
        kp_load.wait()

        @pl.when(owner_here)
        def _():
            kv[my_owner, half, :] = jnp.dot(
                hb[own_slot, half, :], kp[...], preferred_element_type=F32
            ).astype(BF16)
            om[my_owner] = om[2]
            key_cross(my_owner).start()
            for n, to in enumerate((up, down)):
                key_copy(my_owner, n, to).start()
                int_copy(my_owner, n, to).start()

    def hops(o):
        return (z - y - NY * o + 2 * NZ) % NZ

    def key_relay(hop):
        for o in range(2):
            key_relay_of(o, hop)

    def key_relay_of(o, hop):
        @pl.when((hops(o) == hop) | ((hops(o) == NZ - hop) & (hop < 4)))
        def _():
            key_copy(o, 0, up).wait_recv()
            int_copy(o, 0, up).wait_recv()
            key_cross(o).start()

        if hop < 4:
            @pl.when(hops(o) == hop)
            def _():
                key_copy(o, 0, up).start()
                int_copy(o, 0, up).start()

        if hop < 3:
            @pl.when(hops(o) == NZ - hop)
            def _():
                key_copy(o, 1, down).start()
                int_copy(o, 1, down).start()

    def keys_sent(o):
        def sent(ref, sem):
            rcopy(ref, ref, sem, kv_r.at[o], up).wait_send()

        @pl.when(hops(o) == 0)
        def _():
            sent(kv.at[o], kv_s.at[o])
            sent(om.at[0:2], om_s.at[o])

        @pl.when(((hops(o) > 0) & (hops(o) < 4)) | (hops(o) > 5))
        def _():
            sent(kv.at[o, half], kv_s.at[o])
            sent(om.at[o], om_s.at[o])

    def keys_ready():
        for o in range(2):
            key_cross_in(o).wait_recv()

    def tokens_ready():
        rcopy(om.at[2], mt.at[1], mt_s.at[0], mt_r.at[1], right).wait_recv()

        @pl.when(second)
        def _():
            rcopy(om.at[2], mt.at[0], mt_s.at[0], mt_r.at[0], right).wait_recv()

        def turn(blk, _):
            for s in range(2):
                tc[s, blk] = column(s, blk)
                dc[s, blk] = column(s, 6 + blk)
            return 0

        lax.fori_loop(0, 6, turn, 0)

    def memory_ready():
        keys_ready()
        lane = lax.broadcasted_iota(jnp.int32, (1, 128), 1)
        for s in range(2):
            live = lane < mt[s, 14:15, :]
            for o in range(2):
                owner_id = (y + NY * o) * NX + x
                named = live & (mt[s, 12:13, :] == owner_id)
                blocks = mt[s, 13:14, :].astype(F32)
                most = jnp.max(jnp.where(named, blocks, -1.0), axis=1, keepdims=True)
                least = jnp.min(jnp.where(named, blocks, 99.0), axis=1, keepdims=True)
                least = jnp.where(least == most, 99.0, least)
                mine = jnp.where(owner_id == z * NX + tok_x(s), 1.0, 0.0)
                for k, at_block in enumerate((most, least)):
                    n = 2 * o + k
                    keys = jnp.zeros((128, 128), F32)
                    tgts, docs = jnp.zeros((1, 128), F32), jnp.full((1, 128), -1.0, F32)
                    for b in range(6):
                        w = jnp.where(at_block == float(b), 1.0, 0.0)
                        keys = keys + w * kv[o, b * 128 : b * 128 + 128, :].astype(F32)
                        tgts = tgts + w * om[o, b : b + 1, :].astype(F32)
                        docs = docs + w * (om[o, 6 + b : 7 + b, :].astype(F32) + 1.0)
                    kg[s, n * 128 : n * 128 + 128, :] = keys.astype(BF16)
                    kt[s, n : n + 1, :] = tgts
                    kd[s, n : n + 1, :] = docs
                    ko[s, n : n + 1, :] = jnp.broadcast_to(mine * (at_block + 1.0) - 1.0, (1, 128))

    def column(s, row):
        return jnp.broadcast_to(mt[s, pl.ds(row, 1), :].astype(F32), (128, 128)).T

    def rows_at(blk):
        return pl.ds(pl.multiple_of(blk * 128, 128), 128)

    def two_blocks(sa, ba, sb, bb):
        return jnp.concatenate([hb[sa, rows_at(ba), :], hb[sb, rows_at(bb), :]], axis=0)

    def peaks(tiles):
        top = tiles[0]
        for t in tiles[1:]:
            top = jnp.maximum(top, t)
        top = jnp.max(top, axis=1, keepdims=True)
        total = jnp.exp(tiles[0] - top)
        for t in tiles[1:]:
            total = total + jnp.exp(t - top)
        return top, jnp.sum(total, axis=1, keepdims=True)

    def halves(n):
        sa, ba, sb, bb = groups[n]
        return (0, sa, ba), (1, sb, bb)

    def lane_tile(first_lane, columns):
        i1 = lax.broadcasted_iota(jnp.int32, (128, 128), 1)
        t = columns[-1]
        for k in range(len(columns) - 2, -1, -1):
            t = jnp.where(i1 == first_lane + k, columns[k], t)
        return t

    def score_tiles(n):
        q2 = jnp.dot(two_blocks(*groups[n]), kp[...], preferred_element_type=F32).astype(BF16)
        i0 = lax.broadcasted_iota(jnp.int32, (128, 128), 0)
        i1 = lax.broadcasted_iota(jnp.int32, (128, 128), 1)
        eye = i0 == i1
        out_tiles = []
        for h, s, blk in halves(n):
            q = q2[h * 128 : h * 128 + 128]
            tcol, dcol = tc[s, blk], dc[s, blk]
            sc = SCALE * lax.dot_general(q, kg[s], (((1,), (1,)), ((), ())), preferred_element_type=F32)
            kept, hits = [], []
            for m in range(4):
                mine = jnp.where(ko[s, m : m + 1, :] == blk.astype(F32), 2.0, 0.0)
                keep = kd[s, m : m + 1, :] == dcol + jnp.where(eye, mine, 0.0)
                sk = jnp.where(keep, sc[:, m * 128 : m * 128 + 128], NEG)
                kept.append(sk)
                hits.append(jnp.where(kt[s, m : m + 1, :] == tcol, sk, NEG))
            out_tiles.append(lane_tile(4, [*peaks(kept), *peaks(hits)]))
        return out_tiles

    def logit_columns(n, phs):
        a = two_blocks(*groups[n])
        lane = lax.broadcasted_iota(jnp.int32, (1, 128), 1)
        res = [
            (ph, cs, jnp.dot(a, (eb0, eb1)[ph][:, cs * 256 : cs * 256 + 256], preferred_element_type=F32))
            for ph in phs
            for cs in range(2)
        ]
        out_columns = []
        for h, s, blk in halves(n):
            tcol = tc[s, blk]
            tiles, pick = [], None
            for ph, cs, r in res:
                for k in range(2):
                    t = r[h * 128 : h * 128 + 128, k * 128 : k * 128 + 128]
                    base = (2 * y + cs) * 2048 + x * 512 + OFFSET[ph] + k * 128
                    hit = jnp.where((lane + base).astype(F32) == tcol, t, NEG)
                    pick = hit if pick is None else jnp.maximum(pick, hit)
                    tiles.append(t)
            out_columns.append([*peaks(tiles), jnp.max(pick, axis=1, keepdims=True)])
        return out_columns

    def early(n):
        columns = logit_columns(n, (0,))
        memory = score_tiles(n)
        for h in range(2):
            sp[n, h] = lane_tile(8, columns[h])
            sm[n, h] = memory[h]

    def late(was_early, *ns):
        rows = [r for n in ns for r in late_rows(n, was_early)]
        for n, h, s, blk, values in rows:
            for k, row in enumerate(values):
                if n < 5:
                    st[s, k, pl.ds(blk, 1), :] = row
                else:
                    last[s, pl.ds(k + (4 * (1 - c) if h else 0), 1), :] = row

    def late_rows(n, was_early):
        i1 = lax.broadcasted_iota(jnp.int32, (128, 128), 1)
        columns = logit_columns(n, (1,) if was_early else (0, 1))
        memory = [sm[n, 0], sm[n, 1]] if was_early else score_tiles(n)
        rows = []
        for h, s, blk in halves(n):
            t = jnp.where(i1 < 4, lane_tile(0, columns[h]), memory[h])
            if was_early:
                t = jnp.where(i1 < 8, t, sp[n, h])
            t = t.T
            parts = [(t[0:1], t[1:2], t[2:3], 1.0), (t[4:5], t[5:6], t[6:7], t[7:8])]
            if was_early:
                parts.append((t[8:9], t[9:10], t[10:11], 1.0))
            peak, hit = parts[0][0], parts[0][2]
            for lp, _, lh, _ in parts[1:]:
                peak, hit = jnp.maximum(peak, lp), jnp.maximum(hit, lh)
            mass, hmass = None, None
            for lp, lm, lh, hm in parts:
                m, g = lm * jnp.exp(lp - peak), hm * jnp.exp(lh - hit)
                mass = m if mass is None else mass + m
                hmass = g if hmass is None else hmass + g
            rows.append((n, h, s, blk, (peak, mass, hit, hmass)))
        return rows

    def st_send(s, n):
        to = (z * NX + tok_x(s), (v + n) % 8)
        return rcopy(st.at[s], rr.at[(2 * c + s) * NY + y], r_s.at[0], r_r.at[0], to)

    def last_send(s, n):
        to = (z * NX + tok_x(s), (v + n) % 8)
        return rcopy(last.at[s], rl.at[(2 * c + s) * NY + y - 4], rl_s.at[0], rl_r.at[0], to)

    def most_results():
        for n in range(1, 8):
            for s in range(2):
                st_send(s, n).start()
        st_send(1, 0).start()

        @pl.when(second)
        def _():
            st_send(0, 0).start()

        @pl.when(first)
        def _():
            rr[y] = st[0]

    for e in (3, 2, 1):
        xe(0, e).start()
    z_first(0, 0)
    z_first(1, 0)
    x_send(0)
    x_send(1)
    small_sends()
    x_send(2)
    x_send(3)
    for e in (3, 2, 1):
        xe(1, e).start()
    for j in range(4, 12):
        x_send(j)
    key_sends()
    z_first(0, 1)
    z_first(0, 2)

    z_events = [(ph, s, q) for ph in range(2) for s in range(1, 5) for q in range(2 if s < 4 else 1)]
    qy, qd, qu, qo = 2 + y, 2 + (y + 3) % 4, 2 + (y + 1) % 4, 2 + (y + 2) % 4
    plan = {}

    def at(u, fn, *args):
        plan.setdefault(u, []).append((fn, args))

    for n, ev in enumerate(z_events):
        at(n, z_event, *ev)
    for hop, u in ((1, 0), (2, 2), (3, 4), (4, 5)):
        at(u, key_relay, hop)
    at(4.6, z_first, 1, 1)
    at(5.5, z_first, 1, 2)
    for j, u in enumerate((-1, 1, 3, 4, 7, 8, 9, 9.4, 11, 12, 13.2, 13.2)):
        at(u, x_near, j)
    for u, js in ((9.45, (4, 6)), (10.5, (5, 7)), (13.3, (8, 10)), (13.3, (9, 11))):
        at(u, x_forward, *js)
    for u, js in ((4, (0,)), (5, (1,)), (6, (2,)), (8, (3,)), (13.3, (4, 6)), (13.3, (5, 7)), (17, (8, 10)), (18, (9, 11))):
        at(u, x_far, *js)
    for k in range(4):
        at((6, 8, 9, 11.4)[k], y_near, k)
        at((9, 10, 11.4, 12.4)[k], y_far, k)
        at((15, 17, 16, 18)[k], y_last, k)
    groups = [
        [jnp.where(first, a, b) for a, b in zip(on_first, on_second)]
        for on_first, on_second in (
            ((0, 0, 0, 1), (0, qy, 1, qy)),
            ((0, qy, 0, qd), (0, 0, 1, 0)),
            ((0, qu, 0, qo), (0, qd, 1, qd)),
            ((1, qd, 1, qu), (0, qu, 1, qu)),
            ((1, qy, 1, 0), (0, 1, 1, 1)),
            ((1, 1, 1, qo), (0, qo, 1, qo)),
        )
    ]
    at(4, tokens_ready)
    at(7, memory_ready)
    at(7.5, embed_ready, 0)
    at(7.5, early, 0)
    at(9.5, early, 1)
    at(11.5, early, 2)
    at(12.5, early, 3)
    at(13.4, early, 4)
    at(14, embed_ready, 1)
    at(14, late, True, 0, 1)
    at(14, late, True, 2, 3)
    at(15, late, True, 4)
    at(18, late, False, 5)
    at(17, most_results)
    for u in sorted(plan):
        for fn, args in plan[u]:
            fn(*args)

    for n in range(8):
        last_send(1, n).start()

    @pl.when(second)
    def _():
        for n in range(8):
            last_send(0, n).start()

    @pl.when(first)
    def _():
        rcopy(rr.at[0:15], rr.at[0:15], r_s.at[0], r_r.at[0], right).wait_recv()

    @pl.when(second)
    def _():
        rcopy(rr, rr, r_s.at[0], r_r.at[0], right).wait_recv()

    rcopy(rl, rl, rl_s.at[0], rl_r.at[0], right).wait_recv()
    for n in range(4):
        far_blk = 2 + (n + 2) % 4
        for k in range(4):
            rr[4 + n, k, 1:2] = rl[n, k : k + 1]
            rr[4 + n, k, far_blk : far_blk + 1] = rl[n, 4 + k : 5 + k]
            for m in (4, 8):
                rr[4 + m + n, k, far_blk : far_blk + 1] = rl[m + n, k : k + 1]

    peak, hit = rr[0, 0], rr[0, 2]
    for n in range(1, 16):
        peak = jnp.maximum(peak, rr[n, 0])
        hit = jnp.maximum(hit, rr[n, 2])
    mass = rr[0, 1] * jnp.exp(rr[0, 0] - peak)
    hmass = rr[0, 3] * jnp.exp(rr[0, 2] - hit)
    for n in range(1, 16):
        mass = mass + rr[n, 1] * jnp.exp(rr[n, 0] - peak)
        hmass = hmass + rr[n, 3] * jnp.exp(rr[n, 2] - hit)
    loss = peak + jnp.log(mass) - hit - jnp.log(hmass)
    out[...] = loss[0:6]

    def sent(ref, sem):
        rcopy(ref, ref, sem.at[0], dc_r.at[0], right).wait_send()

    sent(hb.at[0, pl.ds(0, 48)], xe_s)
    sent(hb.at[0, pl.ds(0, 448)], z_s)
    sent(hb.at[0, pl.ds(0, 512)], dc_s)
    sent(kv.at[0], kc_s)
    for o in range(2):
        keys_sent(o)

    @pl.when(first)
    def _():
        sent(om, mt_s)
        sent(hb.at[0], hx_s)
        sent(hb.at[0, pl.ds(0, 384)], y_s)
        sent(rr.at[0:15], r_s)
        sent(rl.at[0:8], rl_s)

    @pl.when(second)
    def _():
        sent(hb.at[0, pl.ds(0, 384)], hf_s)
        sent(hb.at[0], y_s)
        sent(rr, r_s)
        sent(tc.at[0, 0:1], rl_s)


def per_device(hidden, out_embed, key_proj, targets, doc_ids, list_owner, list_block, list_count):
    dma = pltpu.SemaphoreType.DMA
    loss = pl.pallas_call(
        kernel,
        out_shape=jax.ShapeDtypeStruct((6, 128), F32),
        in_specs=[pl.BlockSpec(memory_space=pltpu.HBM)] * 5 + [pl.BlockSpec(memory_space=pltpu.VMEM)] * 2 + [pl.BlockSpec(memory_space=pltpu.SMEM)],
        out_specs=pl.BlockSpec(memory_space=pltpu.VMEM),
        scratch_shapes=[
            pltpu.VMEM((3, 768, 4096), BF16),
            pltpu.VMEM((4096, 512), BF16),
            pltpu.VMEM((4096, 512), BF16),
            pltpu.VMEM((4096, 128), BF16),
            pltpu.VMEM((2, 768, 128), BF16),
            pltpu.VMEM((2, 16, 128), jnp.int32),
            pltpu.VMEM((3, 16, 128), jnp.int32),
            pltpu.VMEM((2, 512, 128), BF16),
            pltpu.VMEM((2, 8, 128), F32),
            pltpu.VMEM((2, 8, 128), F32),
            pltpu.VMEM((2, 8, 128), F32),
            pltpu.VMEM((2, 6, 128, 128), F32),
            pltpu.VMEM((2, 6, 128, 128), F32),
            pltpu.VMEM((5, 2, 128, 128), F32),
            pltpu.VMEM((5, 2, 128, 128), F32),
            pltpu.VMEM((2, 4, 8, 128), F32),
            pltpu.VMEM((2, 8, 128), F32),
            pltpu.VMEM((16, 4, 8, 128), F32),
            pltpu.VMEM((12, 8, 128), F32),
            dma((5,)),
            dma((1,)), dma((2, 4)), dma((1,)), dma((2, 4, 4)), dma((1,)), dma((2,)),
            dma((1,)), dma((1,)), dma((12,)), dma((1,)), dma((4,)), dma((4,)),
            dma((2,)), dma((2,)), dma((2,)), dma((2,)), dma((1,)), dma((2,)), dma((1,)), dma((2,)),
            dma((1,)), dma((1,)), dma((1,)), dma((1,)),
        ],
        compiler_params=pltpu.CompilerParams(
            collective_id=0, has_side_effects=True, vmem_limit_bytes=56 * 2**20
        ),
    )(hidden, out_embed, key_proj, targets, doc_ids, list_owner, list_block, list_count)
    return loss.reshape(768)


def solution(mesh):
    placed = (
        P("dp", None),
        P("dp", "vocab"),
        P(),
        P("dp"),
        P("dp"),
        P("dp", None),
        P("dp", None),
        P("dp"),
    )
    return jax.shard_map(per_device, mesh=mesh, in_specs=placed, out_specs=P("dp"), check_vma=False)
```

```python
import jax
import jax.numpy as jnp
from jax import lax
from jax.experimental import pallas as pl
from jax.experimental.pallas import tpu as pltpu
from jax.sharding import PartitionSpec as P

MESH = pl.DeviceIdType.MESH
NEG = -1e30
SCALE = 3.0 / 128**0.5
NX, NY, NZ = 4, 4, 8
CHUNK = 32
F32 = jnp.float32
WIDTH, OFFSET = (256, 256), (0, 256)
BF16 = jnp.bfloat16


def kernel(
    hid, emb, kproj, tgt, doc, lown, lblk, lcnt, out,
    hb, eb0, eb1, kp, kv, mt, om, kg, kt, kd, ko, tc, dc, sp, sm, st, last, rr, rl,
    loc_sem, xe_s, xe_r, z_s, z_r, dc_s, dc_r,
    hx_s, hf_s, hx_r, y_s, y_r, yf_r,
    kv_s, kv_r, om_s, om_r, kc_s, kc_r, mt_s, mt_r, r_s, r_r, rl_s, rl_r,
):
    d = lax.axis_index("dp")
    v = lax.axis_index("vocab")
    z, x = d // NX, d % NX
    y, c = v // 2, v % 2
    owner_here = z % NY == y
    first, second = c == 0, c == 1

    def eb(ph, row, rows, shard):
        w = WIDTH[ph]
        return (eb0, eb1)[ph].at[pl.ds(row, rows), pl.ds(pl.multiple_of(shard * w, 128), w)]

    def tok_x(s):
        return (x + 3 * c + 2 * s) % NX

    def dev(dz, dx, dy, dc):
        return (((z + dz) % NZ) * NX + (x + dx) % NX, ((y + dy) % NY) * 2 + (c + dc) % 2)

    def rcopy(src, dst, ssem, rsem, to):
        return pltpu.make_async_remote_copy(
            src_ref=src, dst_ref=dst, send_sem=ssem, recv_sem=rsem, device_id=to, device_id_type=MESH
        )

    bar = pltpu.get_barrier_semaphore()
    for to in [dev(1, 0, 0, 0), dev(NZ - 1, 0, 0, 0)] + [
        dev(0, 1, 0, 0), dev(0, 2, 0, 0), dev(0, 3, 0, 0), dev(0, 1, 0, 1), dev(0, 3, 0, 1)
    ]:
        pl.semaphore_signal(bar, inc=1, device_id=to, device_id_type=MESH)
    for n in range(1, 8):
        pl.semaphore_signal(bar, inc=1, device_id=(d, (v + n) % 8), device_id_type=MESH)

    om_loads = []
    for n in range(6):
        om_loads.append(pltpu.make_async_copy(tgt.at[pl.ds(n * 128, 128)], om.at[2, n], loc_sem.at[4]))
        om_loads.append(pltpu.make_async_copy(doc.at[pl.ds(n * 128, 128)], om.at[2, 6 + n], loc_sem.at[4]))
    for cp in om_loads:
        cp.start()
    emb_loads = []
    for ph in range(2):
        col = pl.multiple_of(x * 512 + OFFSET[ph], 128)
        cp = pltpu.make_async_copy(
            emb.at[:, pl.ds(col, WIDTH[ph])], eb(ph, pl.multiple_of(d * 128, 128), 128, c), loc_sem.at[2 + ph]
        )
        cp.start()
        emb_loads.append(cp)
    own_slot = 2 * c
    kp_load = pltpu.make_async_copy(kproj, kp, loc_sem.at[1])
    kp_load.start()
    hid_load = pltpu.make_async_copy(hid, hb.at[own_slot], loc_sem.at[0])
    hid_load.start()
    om[2, 12:16] = jnp.zeros((4, 128), jnp.int32)
    om[2, 12:13, 0:64] = lown[...]
    om[2, 13:14, 0:64] = lblk[...]
    om[2, 14:15] = jnp.full((1, 128), lcnt[0], jnp.int32)
    pl.semaphore_wait(bar, 14)

    def eslot(ph, zz, i):
        row = ((zz % NZ) * NX + (x + i) % NX) * 128
        return eb(ph, pl.multiple_of(row, 128), 128, c)

    def xe(ph, e):
        col = pl.multiple_of(((x + e) % NX) * 512 + OFFSET[ph], 128)
        return rcopy(
            emb.at[:, pl.ds(col, WIDTH[ph])],
            eb(ph, pl.multiple_of(d * 128, 128), 128, c),
            xe_s.at[0], xe_r.at[ph, 4 - e], dev(0, e, 0, 0),
        )

    def xe_in(ph, i):
        return rcopy(
            emb.at[:, pl.ds(0, WIDTH[ph])], eslot(ph, z, i), xe_s.at[0], xe_r.at[ph, i], dev(0, i, 0, 0)
        )

    def zplus(ph, s, i):
        ref = eslot(ph, z - (s - 1) + NZ, i)
        return rcopy(ref, ref, z_s.at[0], z_r.at[ph, s - 1, i], dev(1, 0, 0, 0))

    def zminus(ph, s, i):
        ref = eslot(ph, z + (s - 1), i)
        return rcopy(ref, ref, z_s.at[0], z_r.at[ph, s - 1, i - 2 if s == 4 else i], dev(NZ - 1, 0, 0, 0))

    def z_in(ph, s, i):
        ref = eb(ph, 0, 256, c)
        return rcopy(ref, ref, z_s.at[0], z_r.at[ph, s - 1, i], dev(1, 0, 0, 0))

    def d2d(ph, zz, n, shard):
        ref = eb(ph, pl.multiple_of((zz % NZ) * 512, 512), 512, shard)
        return rcopy(ref, ref, dc_s.at[0], dc_r.at[ph], dev(0, 0, 0, 1))

    d2d_z = [0, 7, 6, 5, 1, 2, 3, 4]

    def z_first(ph, pair):
        for i in ((0,), (1,), (2, 3))[pair]:
            if i == 0:
                emb_loads[ph].wait()
            else:
                xe_in(ph, i).wait_recv()
            zplus(ph, 1, i).start()
            zminus(ph, 1, i).start()
        if pair == 2:
            d2d(ph, z, 0, c).start()

    def z_event(ph, s, pair):
        if s < 4:
            for i in (0, 1) if pair == 0 else (2, 3):
                z_in(ph, s, i).wait_recv()
                if s < 3 or i < 2:
                    zplus(ph, s + 1, i).start()
                if s < 3 or i >= 2:
                    zminus(ph, s + 1, i).start()
            if pair == 1:
                d2d(ph, z + NZ - s, s, c).start()
                d2d(ph, z + s, 3 + s, c).start()
        else:
            for i in (0, 1):
                z_in(ph, 4, i).wait_recv()
            d2d(ph, z + 4, 7, c).start()

    def embed_ready(ph):
        ref = eb(ph, 0, 4096, 1 - c)
        rcopy(ref, ref, dc_s.at[0], dc_r.at[ph], dev(0, 0, 0, 1)).wait_recv()

    def rows_of(j, yy):
        b, k = j // 4, j % 4
        if b == 0:
            return pl.ds(pl.multiple_of(256 + (yy % NY) * 128 + k * CHUNK, CHUNK), CHUNK)
        return pl.ds((b - 1) * 128 + k * CHUNK, CHUNK)

    right, left = dev(0, 1, 0, 1), dev(0, 3, 0, 1)

    def hx_own(j, s):
        r = rows_of(j, y)
        return rcopy(hid.at[r], hb.at[s, r], hx_s.at[0], hx_r.at[j], (right, left)[s])

    def hx_fwd(j):
        r = rows_of(j, y)
        s = 0 if j % 4 < 2 else 1
        return rcopy(hb.at[s, r], hb.at[1, r], hf_s.at[0], hx_r.at[j], (right, left)[s])

    def arrived(sem, rows):
        ref = hb.at[0, pl.ds(0, rows)]
        rcopy(ref, ref, hf_s.at[0], sem, right).wait_recv()

    def yown(s, k, up):
        r = rows_of(k, y)
        if up:
            return rcopy(hb.at[s, r], hb.at[s, r], y_s.at[0], y_r.at[k], dev(0, 0, 1, 0))
        return rcopy(hb.at[s, r], hb.at[s, r], y_s.at[0], y_r.at[k], dev(0, 0, 3, 0))

    def yfwd(s, k):
        if k < 2:
            r = rows_of(k, y + 3)
            return rcopy(hb.at[s, r], hb.at[s, r], y_s.at[0], yf_r.at[k], dev(0, 0, 1, 0))
        r = rows_of(k, y + 1)
        return rcopy(hb.at[s, r], hb.at[s, r], y_s.at[0], yf_r.at[k], dev(0, 0, 3, 0))

    def x_send(j):
        @pl.when(first)
        def _():
            hx_own(j, 0).start()
            hx_own(j, 1).start()

    def x_near(j):
        @pl.when(second)
        def _():
            arrived(hx_r.at[j], 64)
            if j < 4:
                hx_fwd(j).start()
                for s in range(2):
                    yown(s, j, True).start()
                    yown(s, j, False).start()

    def x_forward(*js):
        @pl.when(second)
        def _():
            for j in js:
                hx_fwd(j).start()

    def x_far(*js):
        @pl.when(first)
        def _():
            for j in js:
                arrived(hx_r.at[j], 32)
                if j < 4:
                    yown(1, j, True).start()
                    yown(1, j, False).start()

    def y_near(k):
        @pl.when(second)
        def _():
            arrived(y_r.at[k], 128)
            yfwd(0, k).start()
            yfwd(1, k).start()

    def y_far(k):
        @pl.when(first)
        def _():
            arrived(y_r.at[k], 64)
            yfwd(1, k).start()

    def y_last(k):
        @pl.when(first)
        def _():
            arrived(yf_r.at[k], 32)

        @pl.when(second)
        def _():
            arrived(yf_r.at[k], 64)

    my_owner = z // NY
    half = pl.ds(pl.multiple_of(c * 384, 384), 384)
    up, down = dev(1, 0, 0, 0), dev(NZ - 1, 0, 0, 0)

    def key_copy(o, n, to):
        return rcopy(kv.at[o, half], kv.at[o, half], kv_s.at[o], kv_r.at[o], to)

    def int_copy(o, n, to):
        return rcopy(om.at[o], om.at[o], om_s.at[o], om_r.at[o], to)

    def key_cross(o):
        return rcopy(kv.at[o, half], kv.at[o, half], kc_s.at[0], kc_r.at[o], dev(0, 0, 0, 1))

    def key_cross_in(o):
        ref = kv.at[o, pl.ds(pl.multiple_of(384 - c * 384, 384), 384)]
        return rcopy(ref, ref, kc_s.at[0], kc_r.at[o], dev(0, 0, 0, 1))

    def mt_send(n):
        to, s = ((dev(0, 2, 0, 0), 1), (right, 0), (left, 1))[n]
        return rcopy(om.at[2], mt.at[s], mt_s.at[0], mt_r.at[s], to)

    def small_sends():
        for cp in om_loads:
            cp.wait()

        @pl.when(first)
        def _():
            for n in range(3):
                mt_send(n).start()
            mt[0] = om[2]

    def key_sends():
        hid_load.wait()
        kp_load.wait()

        @pl.when(owner_here)
        def _():
            kv[my_owner, half, :] = jnp.dot(
                hb[own_slot, half, :], kp[...], preferred_element_type=F32
            ).astype(BF16)
            om[my_owner] = om[2]
            key_cross(my_owner).start()
            for n, to in enumerate((up, down)):
                key_copy(my_owner, n, to).start()
                int_copy(my_owner, n, to).start()

    def hops(o):
        return (z - y - NY * o + 2 * NZ) % NZ

    def key_relay(hop):
        for o in range(2):
            key_relay_of(o, hop)

    def key_relay_of(o, hop):
        @pl.when((hops(o) == hop) | ((hops(o) == NZ - hop) & (hop < 4)))
        def _():
            key_copy(o, 0, up).wait_recv()
            int_copy(o, 0, up).wait_recv()
            key_cross(o).start()

        if hop < 4:
            @pl.when(hops(o) == hop)
            def _():
                key_copy(o, 0, up).start()
                int_copy(o, 0, up).start()

        if hop < 3:
            @pl.when(hops(o) == NZ - hop)
            def _():
                key_copy(o, 1, down).start()
                int_copy(o, 1, down).start()

    def keys_sent(o):
        def sent(ref, sem):
            rcopy(ref, ref, sem, kv_r.at[o], up).wait_send()

        @pl.when(hops(o) == 0)
        def _():
            sent(kv.at[o], kv_s.at[o])
            sent(om.at[0:2], om_s.at[o])

        @pl.when(((hops(o) > 0) & (hops(o) < 4)) | (hops(o) > 5))
        def _():
            sent(kv.at[o, half], kv_s.at[o])
            sent(om.at[o], om_s.at[o])

    def keys_ready():
        for o in range(2):
            key_cross_in(o).wait_recv()

    def tokens_ready():
        rcopy(om.at[2], mt.at[1], mt_s.at[0], mt_r.at[1], right).wait_recv()

        @pl.when(second)
        def _():
            rcopy(om.at[2], mt.at[0], mt_s.at[0], mt_r.at[0], right).wait_recv()

        def turn(blk, _):
            for s in range(2):
                tc[s, blk] = column(s, blk)
                dc[s, blk] = column(s, 6 + blk)
            return 0

        lax.fori_loop(0, 6, turn, 0)

    def memory_ready():
        keys_ready()
        lane = lax.broadcasted_iota(jnp.int32, (1, 128), 1)
        for s in range(2):
            live = lane < mt[s, 14:15, :]
            for o in range(2):
                owner_id = (y + NY * o) * NX + x
                named = live & (mt[s, 12:13, :] == owner_id)
                blocks = mt[s, 13:14, :].astype(F32)
                most = jnp.max(jnp.where(named, blocks, -1.0), axis=1, keepdims=True)
                least = jnp.min(jnp.where(named, blocks, 99.0), axis=1, keepdims=True)
                least = jnp.where(least == most, 99.0, least)
                mine = jnp.where(owner_id == z * NX + tok_x(s), 1.0, 0.0)
                for k, at_block in enumerate((most, least)):
                    n = 2 * o + k
                    keys = jnp.zeros((128, 128), F32)
                    tgts, docs = jnp.zeros((1, 128), F32), jnp.full((1, 128), -1.0, F32)
                    for b in range(6):
                        w = jnp.where(at_block == float(b), 1.0, 0.0)
                        keys = keys + w * kv[o, b * 128 : b * 128 + 128, :].astype(F32)
                        tgts = tgts + w * om[o, b : b + 1, :].astype(F32)
                        docs = docs + w * (om[o, 6 + b : 7 + b, :].astype(F32) + 1.0)
                    kg[s, n * 128 : n * 128 + 128, :] = keys.astype(BF16)
                    kt[s, n : n + 1, :] = tgts
                    kd[s, n : n + 1, :] = docs
                    ko[s, n : n + 1, :] = jnp.broadcast_to(mine * (at_block + 1.0) - 1.0, (1, 128))

    def column(s, row):
        return jnp.broadcast_to(mt[s, pl.ds(row, 1), :].astype(F32), (128, 128)).T

    def rows_at(blk):
        return pl.ds(pl.multiple_of(blk * 128, 128), 128)

    def two_blocks(sa, ba, sb, bb):
        return jnp.concatenate([hb[sa, rows_at(ba), :], hb[sb, rows_at(bb), :]], axis=0)

    def peaks(tiles):
        top = tiles[0]
        for t in tiles[1:]:
            top = jnp.maximum(top, t)
        top = jnp.max(top, axis=1, keepdims=True)
        total = jnp.exp(tiles[0] - top)
        for t in tiles[1:]:
            total = total + jnp.exp(t - top)
        return top, jnp.sum(total, axis=1, keepdims=True)

    def halves(n):
        sa, ba, sb, bb = groups[n]
        return (0, sa, ba), (1, sb, bb)

    def lane_tile(first_lane, columns):
        i1 = lax.broadcasted_iota(jnp.int32, (128, 128), 1)
        t = columns[-1]
        for k in range(len(columns) - 2, -1, -1):
            t = jnp.where(i1 == first_lane + k, columns[k], t)
        return t

    def score_tiles(n):
        q2 = jnp.dot(two_blocks(*groups[n]), kp[...], preferred_element_type=F32).astype(BF16)
        i0 = lax.broadcasted_iota(jnp.int32, (128, 128), 0)
        i1 = lax.broadcasted_iota(jnp.int32, (128, 128), 1)
        eye = i0 == i1
        out_tiles = []
        for h, s, blk in halves(n):
            q = q2[h * 128 : h * 128 + 128]
            tcol, dcol = tc[s, blk], dc[s, blk]
            sc = SCALE * lax.dot_general(q, kg[s], (((1,), (1,)), ((), ())), preferred_element_type=F32)
            kept, hits = [], []
            for m in range(4):
                mine = jnp.where(ko[s, m : m + 1, :] == blk.astype(F32), 2.0, 0.0)
                keep = kd[s, m : m + 1, :] == dcol + jnp.where(eye, mine, 0.0)
                sk = jnp.where(keep, sc[:, m * 128 : m * 128 + 128], NEG)
                kept.append(sk)
                hits.append(jnp.where(kt[s, m : m + 1, :] == tcol, sk, NEG))
            out_tiles.append(lane_tile(4, [*peaks(kept), *peaks(hits)]))
        return out_tiles

    def logit_columns(n, phs):
        a = two_blocks(*groups[n])
        lane = lax.broadcasted_iota(jnp.int32, (1, 128), 1)
        res = [
            (ph, cs, jnp.dot(a, (eb0, eb1)[ph][:, cs * 256 : cs * 256 + 256], preferred_element_type=F32))
            for ph in phs
            for cs in range(2)
        ]
        out_columns = []
        for h, s, blk in halves(n):
            tcol = tc[s, blk]
            tiles, pick = [], None
            for ph, cs, r in res:
                for k in range(2):
                    t = r[h * 128 : h * 128 + 128, k * 128 : k * 128 + 128]
                    base = (2 * y + cs) * 2048 + x * 512 + OFFSET[ph] + k * 128
                    hit = jnp.where((lane + base).astype(F32) == tcol, t, NEG)
                    pick = hit if pick is None else jnp.maximum(pick, hit)
                    tiles.append(t)
            out_columns.append([*peaks(tiles), jnp.max(pick, axis=1, keepdims=True)])
        return out_columns

    def early(n):
        memory = score_tiles(n)
        columns = logit_columns(n, (0,))
        for h in range(2):
            sp[n, h] = lane_tile(8, columns[h])
            sm[n, h] = memory[h]

    def late(was_early, *ns):
        rows = [r for n in ns for r in late_rows(n, was_early)]
        for n, h, s, blk, values in rows:
            for k, row in enumerate(values):
                if n < 5:
                    st[s, k, pl.ds(blk, 1), :] = row
                else:
                    last[s, pl.ds(k + (4 * (1 - c) if h else 0), 1), :] = row

    def late_rows(n, was_early):
        i1 = lax.broadcasted_iota(jnp.int32, (128, 128), 1)
        memory = [sm[n, 0], sm[n, 1]] if was_early else score_tiles(n)
        columns = logit_columns(n, (1,) if was_early else (0, 1))
        rows = []
        for h, s, blk in halves(n):
            t = jnp.where(i1 < 4, lane_tile(0, columns[h]), memory[h])
            if was_early:
                t = jnp.where(i1 < 8, t, sp[n, h])
            t = t.T
            parts = [(t[0:1], t[1:2], t[2:3], 1.0), (t[4:5], t[5:6], t[6:7], t[7:8])]
            if was_early:
                parts.append((t[8:9], t[9:10], t[10:11], 1.0))
            peak, hit = parts[0][0], parts[0][2]
            for lp, _, lh, _ in parts[1:]:
                peak, hit = jnp.maximum(peak, lp), jnp.maximum(hit, lh)
            mass, hmass = None, None
            for lp, lm, lh, hm in parts:
                m, g = lm * jnp.exp(lp - peak), hm * jnp.exp(lh - hit)
                mass = m if mass is None else mass + m
                hmass = g if hmass is None else hmass + g
            rows.append((n, h, s, blk, (peak, mass, hit, hmass)))
        return rows

    def st_send(s, n):
        to = (z * NX + tok_x(s), (v + n) % 8)
        return rcopy(st.at[s], rr.at[(2 * c + s) * NY + y], r_s.at[0], r_r.at[0], to)

    def last_send(s, n):
        to = (z * NX + tok_x(s), (v + n) % 8)
        return rcopy(last.at[s], rl.at[(2 * c + s) * NY + y - 4], rl_s.at[0], rl_r.at[0], to)

    def most_results():
        for n in range(1, 8):
            for s in range(2):
                st_send(s, n).start()
        st_send(1, 0).start()

        @pl.when(second)
        def _():
            st_send(0, 0).start()

        @pl.when(first)
        def _():
            rr[y] = st[0]

    for e in (3, 2, 1):
        xe(0, e).start()
    z_first(0, 0)
    z_first(1, 0)
    x_send(0)
    x_send(1)
    small_sends()
    x_send(2)
    x_send(3)
    for e in (3, 2, 1):
        xe(1, e).start()
    for j in range(4, 12):
        x_send(j)
    key_sends()
    z_first(0, 1)
    z_first(0, 2)

    z_events = [(ph, s, q) for ph in range(2) for s in range(1, 5) for q in range(2 if s < 4 else 1)]
    qy, qd, qu, qo = 2 + y, 2 + (y + 3) % 4, 2 + (y + 1) % 4, 2 + (y + 2) % 4
    plan = {}

    def at(u, fn, *args):
        plan.setdefault(u, []).append((fn, args))

    for n, ev in enumerate(z_events):
        at(n, z_event, *ev)
    for hop, u in ((1, 0), (2, 2), (3, 4), (4, 5)):
        at(u, key_relay, hop)
    at(4.6, z_first, 1, 1)
    at(5.5, z_first, 1, 2)
    for j, u in enumerate((-1, 1, 3, 4, 7, 8, 9, 9.4, 11, 12, 13.2, 13.2)):
        at(u, x_near, j)
    for u, js in ((9.45, (4, 6)), (10.5, (5, 7)), (13.3, (8, 10)), (13.3, (9, 11))):
        at(u, x_forward, *js)
    for u, js in ((4, (0,)), (5, (1,)), (6, (2,)), (8, (3,)), (13.3, (4, 6)), (13.3, (5, 7)), (17, (8, 10)), (18, (9, 11))):
        at(u, x_far, *js)
    for k in range(4):
        at((6, 8, 9, 11.4)[k], y_near, k)
        at((9, 10, 11.4, 12.4)[k], y_far, k)
        at((15, 17, 16, 18)[k], y_last, k)
    groups = [
        [jnp.where(first, a, b) for a, b in zip(on_first, on_second)]
        for on_first, on_second in (
            ((0, 0, 0, 1), (0, qy, 1, qy)),
            ((0, qy, 0, qd), (0, 0, 1, 0)),
            ((0, qu, 0, qo), (0, qd, 1, qd)),
            ((1, qd, 1, qu), (0, qu, 1, qu)),
            ((1, qy, 1, 0), (0, 1, 1, 1)),
            ((1, 1, 1, qo), (0, qo, 1, qo)),
        )
    ]
    at(4, tokens_ready)
    at(7, memory_ready)
    at(7.5, embed_ready, 0)
    at(7.5, early, 0)
    at(9.5, early, 1)
    at(11.5, early, 2)
    at(12.5, early, 3)
    at(13.4, early, 4)
    at(14, embed_ready, 1)
    at(14, late, True, 0, 1)
    at(14, late, True, 2, 3)
    at(15, late, True, 4)
    at(18, late, False, 5)
    at(17, most_results)
    for u in sorted(plan):
        for fn, args in plan[u]:
            fn(*args)

    for n in range(8):
        last_send(1, n).start()

    @pl.when(second)
    def _():
        for n in range(8):
            last_send(0, n).start()

    @pl.when(first)
    def _():
        rcopy(rr.at[0:15], rr.at[0:15], r_s.at[0], r_r.at[0], right).wait_recv()

    @pl.when(second)
    def _():
        rcopy(rr, rr, r_s.at[0], r_r.at[0], right).wait_recv()

    rcopy(rl, rl, rl_s.at[0], rl_r.at[0], right).wait_recv()
    for n in range(4):
        far_blk = 2 + (n + 2) % 4
        for k in range(4):
            rr[4 + n, k, 1:2] = rl[n, k : k + 1]
            rr[4 + n, k, far_blk : far_blk + 1] = rl[n, 4 + k : 5 + k]
            for m in (4, 8):
                rr[4 + m + n, k, far_blk : far_blk + 1] = rl[m + n, k : k + 1]

    peak, hit = rr[0, 0], rr[0, 2]
    for n in range(1, 16):
        peak = jnp.maximum(peak, rr[n, 0])
        hit = jnp.maximum(hit, rr[n, 2])
    mass = rr[0, 1] * jnp.exp(rr[0, 0] - peak)
    hmass = rr[0, 3] * jnp.exp(rr[0, 2] - hit)
    for n in range(1, 16):
        mass = mass + rr[n, 1] * jnp.exp(rr[n, 0] - peak)
        hmass = hmass + rr[n, 3] * jnp.exp(rr[n, 2] - hit)
    loss = peak + jnp.log(mass) - hit - jnp.log(hmass)
    out[...] = loss[0:6]

    def sent(ref, sem):
        rcopy(ref, ref, sem.at[0], dc_r.at[0], right).wait_send()

    sent(hb.at[0, pl.ds(0, 48)], xe_s)
    sent(hb.at[0, pl.ds(0, 448)], z_s)
    sent(hb.at[0, pl.ds(0, 512)], dc_s)
    sent(kv.at[0], kc_s)
    for o in range(2):
        keys_sent(o)

    @pl.when(first)
    def _():
        sent(om, mt_s)
        sent(hb.at[0], hx_s)
        sent(hb.at[0, pl.ds(0, 384)], y_s)
        sent(rr.at[0:15], r_s)
        sent(rl.at[0:8], rl_s)

    @pl.when(second)
    def _():
        sent(hb.at[0, pl.ds(0, 384)], hf_s)
        sent(hb.at[0], y_s)
        sent(rr, r_s)
        sent(tc.at[0, 0:1], rl_s)


def per_device(hidden, out_embed, key_proj, targets, doc_ids, list_owner, list_block, list_count):
    dma = pltpu.SemaphoreType.DMA
    loss = pl.pallas_call(
        kernel,
        out_shape=jax.ShapeDtypeStruct((6, 128), F32),
        in_specs=[pl.BlockSpec(memory_space=pltpu.HBM)] * 5 + [pl.BlockSpec(memory_space=pltpu.VMEM)] * 2 + [pl.BlockSpec(memory_space=pltpu.SMEM)],
        out_specs=pl.BlockSpec(memory_space=pltpu.VMEM),
        scratch_shapes=[
            pltpu.VMEM((3, 768, 4096), BF16),
            pltpu.VMEM((4096, 512), BF16),
            pltpu.VMEM((4096, 512), BF16),
            pltpu.VMEM((4096, 128), BF16),
            pltpu.VMEM((2, 768, 128), BF16),
            pltpu.VMEM((2, 16, 128), jnp.int32),
            pltpu.VMEM((3, 16, 128), jnp.int32),
            pltpu.VMEM((2, 512, 128), BF16),
            pltpu.VMEM((2, 8, 128), F32),
            pltpu.VMEM((2, 8, 128), F32),
            pltpu.VMEM((2, 8, 128), F32),
            pltpu.VMEM((2, 6, 128, 128), F32),
            pltpu.VMEM((2, 6, 128, 128), F32),
            pltpu.VMEM((5, 2, 128, 128), F32),
            pltpu.VMEM((5, 2, 128, 128), F32),
            pltpu.VMEM((2, 4, 8, 128), F32),
            pltpu.VMEM((2, 8, 128), F32),
            pltpu.VMEM((16, 4, 8, 128), F32),
            pltpu.VMEM((12, 8, 128), F32),
            dma((5,)),
            dma((1,)), dma((2, 4)), dma((1,)), dma((2, 4, 4)), dma((1,)), dma((2,)),
            dma((1,)), dma((1,)), dma((12,)), dma((1,)), dma((4,)), dma((4,)),
            dma((2,)), dma((2,)), dma((2,)), dma((2,)), dma((1,)), dma((2,)), dma((1,)), dma((2,)),
            dma((1,)), dma((1,)), dma((1,)), dma((1,)),
        ],
        compiler_params=pltpu.CompilerParams(
            collective_id=0, has_side_effects=True, vmem_limit_bytes=56 * 2**20
        ),
    )(hidden, out_embed, key_proj, targets, doc_ids, list_owner, list_block, list_count)
    return loss.reshape(768)


def solution(mesh):
    placed = (
        P("dp", None),
        P("dp", "vocab"),
        P(),
        P("dp"),
        P("dp"),
        P("dp", None),
        P("dp", None),
        P("dp"),
    )
    return jax.shard_map(per_device, mesh=mesh, in_specs=placed, out_specs=P("dp"), check_vma=False)
```
